512 devices in a mesh: node: 16 (over y, core), local: 8 (over z), section: 4 (over x).
Axes of the slice: x: 4, y: 8, z: 8, core: 2. Of those that a mesh axis runs over, the one named last changes fastest.
Arguments:
- inputs_b: bfloat16 [4, 2048, 4096], P('section', 'node', 'local'), may hold values from -6 to 6
- grads_a: bfloat16 [4, 2048, 4096], P('section', 'node', 'local'), may hold values from -6 to 6
- experts_a: int32 [4, 2048, 4], P('section', 'node'), may hold values from 0 to 15, all different within a row; in each aligned block of 128 rows (0 to 127, 128 to 255, ..., all dimensions but the last counted through in order) at most 40 rows name the same one
- experts_b: int32 [4, 2048, 4], P('section', 'node'), may hold values from 0 to 15, all different within a row; in each aligned block of 128 rows (0 to 127, 128 to 255, ..., all dimensions but the last counted through in order) at most 40 rows name the same one
- gates_a: float32 [4, 2048, 4], P('section', 'node'), may hold values from 0.05 to 0.5
- gates_b: float32 [4, 2048, 4], P('section', 'node'), may hold values from 0.05 to 0.5
- w_gate_up: bfloat16 [4, 16, 4096, 2, 1024], P('section', 'node', 'local'), may hold values from -0.09375 to 0.09375
- w_down: bfloat16 [4, 16, 1024, 4096], P('section', 'node', None, 'local'), may hold values from -0.1875 to 0.1875
- saved_a: bfloat16 [4, 16, 2, 1024, 640], P('section', 'node', None, 'local'), may hold values from -5 to 5
Outputs:
- outputs_b: bfloat16 [4, 2048, 4096], P('section', 'node', 'local')
- grads_prev: bfloat16 [4, 2048, 4096], P('section', 'node', 'local')
The draws below stay inside these ranges and needn't reach their ends.
Inputs may be any that keep to these rules, and one draw needn't show every extreme that they name: `experts_a`: each row names 4 distinct experts. Among the 128 rows of one source block of a section, no expert is named by more than 40 rows, and in some blocks an expert is named by exactly 40. `experts_b`: each row names 4 distinct experts. Among the 128 rows of one source block of a section, no expert is named by more than 40 rows, and in some blocks an expert is named by exactly 40.
All inputs are finite; a program needn't handle non-finite values.
Results may differ from the reference program's by a relative error of at most 0.029.
Values may be sent and summed in bfloat16 or wider, within the bound.
No kernel may reach another device: no remote copies, remote signals or barrier semaphores. Data moves between devices by JAX's collectives and lax.ppermute only.
A program may use at most 64 MiB of HBM per device.

```python
import math
import jax
import jax.numpy as jnp
import numpy as np
from jax import lax

D = 4096
FF = 1024
TOK_NODE = 128
TOPK = 4
EXPERTS = 16
CAP = 40
SOURCES = 16
SLOTS = 640
TOKENS = 2048
SECTIONS = 4
N_LOCAL = 8


def steps_of(key, shape, pieces, low, high):
    def one(dim, blocks):
        steps = jax.random.uniform(jax.random.fold_in(jax.random.fold_in(key, 6), dim), (blocks,), jnp.float32, low / len(pieces), high / len(pieces))
        return jnp.repeat(jnp.exp(steps), shape[dim] // blocks).reshape((-1,) + (1,) * (len(shape) - dim - 1))

    gain = one(*pieces[0])
    for cut in pieces[1:]:
        gain = gain * one(*cut)
    return gain


def shared_out(stream_key, own, number, rows, amount, top, limit, skew):
    ranking = jax.random.permutation(stream_key, amount)
    crowded, common = shares(amount, rows * top, limit, skew, True), shares(amount, rows * top, limit, skew, False)
    places = jnp.arange(amount)

    def named(tallies, offset_by):
        used = int((tallies > 0).sum())
        fixed = max(1, used // 4)
        passed = fixed + (places - fixed + offset_by * (used - fixed)) % max(1, amount - fixed)
        return jnp.zeros((amount,), jnp.int32).at[ranking[jnp.where(places < fixed, places, passed)]].set(jnp.asarray(tallies, jnp.int32))

    tallies = jnp.where(number % 4 == 0, named(crowded, number // 4), named(common, number - number // 4 - 1))
    mixed = jax.random.permutation(jax.random.fold_in(own, 3), amount)
    donor, receiver = mixed[0:amount // 2 * 2:2], mixed[1:amount // 2 * 2:2]
    margin = jnp.minimum(tallies[donor] - 1, limit - tallies[receiver]) // 2
    margin = jnp.where((donor == ranking[0]) | (receiver == ranking[0]) | (tallies[receiver] == 0), 0, jnp.maximum(margin, 0))
    passed = jax.random.randint(jax.random.fold_in(own, 4), (amount // 2,), 0, 1 << 20) % (margin + 1)
    tallies = tallies.at[donor].add(-passed).at[receiver].add(passed)
    members = jnp.searchsorted(jnp.cumsum(tallies), jnp.arange(rows * top), side="right").astype(jnp.int32)
    grid = members.reshape(top, rows).T
    grid = grid[jax.random.permutation(jax.random.fold_in(own, 1), rows)]
    offset_by = jax.random.randint(jax.random.fold_in(own, 2), (rows, 1), 0, top)
    return jnp.take_along_axis(grid, (jnp.arange(top)[None, :] + offset_by) % top, axis=1)


def shares(count, total, limit, skew, full):
    weights = [(1 << 20) // math.isqrt(rank ** skew) + 1 for rank in range(1, count + 1)]
    largest = limit if full else min(limit, max(-(-total // count), total * weights[0] // sum(weights)))
    least = 1 if total - largest >= count - 1 else 0
    counts, surplus = [largest] + [least] * (count - 1), total - largest - least * (count - 1)
    while surplus > 0:
        movable = [i for i in range(1, count) if counts[i] < largest] or [i for i in range(1, count) if counts[i] < limit]
        pool, left = sum([weights[i] for i in movable]), surplus
        for i in movable:
            addition = min(limit - counts[i], max(1, left * weights[i] // pool), surplus)
            counts[i] = counts[i] + addition
            surplus = surplus - addition
    return np.array(counts)


def bell_draw(own_key, extent, scale, most, split=(), held_as=jnp.bfloat16):
    result = jax.random.normal(own_key, extent, jnp.float32) * scale
    if len(split) > 0:
        result = steps_of(own_key, extent, split, -0.22, 0.18) * result
    return jnp.clip(result, min=-most, max=most).astype(held_as)


def setup_inputs(seed: int = 0) -> dict:
    key_list = jax.random.split(jax.random.key(seed), 10)
    inputs_b = bell_draw(key_list[0], (SECTIONS, TOKENS, D), 1.0, 6.0, ((0, 4), (1, 16), (2, 8)))
    grads_a = bell_draw(key_list[1], (SECTIONS, TOKENS, D), 1.0, 6.0, ((0, 4), (1, 16), (2, 8)))
    experts_a_keys = jax.random.split(jax.random.fold_in(key_list[2], 1), SECTIONS * TOKENS // TOK_NODE)
    experts_a_turns = jax.random.permutation(jax.random.fold_in(key_list[2], 3), SECTIONS * TOKENS // TOK_NODE)
    experts_a = jax.vmap(lambda own, number: shared_out(jax.random.fold_in(key_list[2], 2), own, number, TOK_NODE, EXPERTS, TOPK, CAP, 2))(experts_a_keys, experts_a_turns).reshape((SECTIONS, TOKENS, TOPK))
    experts_b_keys = jax.random.split(jax.random.fold_in(key_list[3], 1), SECTIONS * TOKENS // TOK_NODE)
    experts_b_turns = jax.random.permutation(jax.random.fold_in(key_list[3], 3), SECTIONS * TOKENS // TOK_NODE)
    experts_b = jax.vmap(lambda own, number: shared_out(jax.random.fold_in(key_list[3], 2), own, number, TOK_NODE, EXPERTS, TOPK, CAP, 2))(experts_b_keys, experts_b_turns).reshape((SECTIONS, TOKENS, TOPK))
    gates_a = jnp.clip(jnp.exp(math.log(0.5) - 2.3025851 * jax.random.uniform(key_list[4], (SECTIONS, TOKENS, TOPK), jnp.float32) ** steps_of(key_list[4], (SECTIONS, TOKENS, TOPK), ((0, 4), (1, 16)), -0.2, 0.2)), 0.05, 0.5)
    gates_b = jnp.clip(jnp.exp(math.log(0.5) - 2.3025851 * jax.random.uniform(key_list[5], (SECTIONS, TOKENS, TOPK), jnp.float32) ** steps_of(key_list[5], (SECTIONS, TOKENS, TOPK), ((0, 4), (1, 16)), -0.2, 0.2)), 0.05, 0.5)
    w_gate_up = bell_draw(key_list[6], (SECTIONS, EXPERTS, D, 2, FF), D ** -0.5, 0.09375, ((0, 4), (1, 16), (2, 8)))
    w_down = bell_draw(key_list[7], (SECTIONS, EXPERTS, FF, D), FF ** -0.5, 0.1875, ((0, 4), (1, 16), (3, 8)))
    saved_a = bell_draw(key_list[8], (SECTIONS, EXPERTS, 2, FF, SLOTS), 1.0, 5.0, ((0, 4), (1, 16), (3, 8)))
    return {"inputs_b": inputs_b, "grads_a": grads_a, "experts_a": experts_a, "experts_b": experts_b, "gates_a": gates_a, "gates_b": gates_b, "w_gate_up": w_gate_up, "w_down": w_down, "saved_a": saved_a}


def slot_layout(ids):
    flat = ids.reshape(SOURCES, TOK_NODE * TOPK)
    onehot = (flat[:, :, None] == jnp.arange(EXPERTS, dtype=jnp.int32)[None, None, :]).astype(jnp.int32)
    before = jnp.cumsum(onehot, axis=1) - onehot
    position = jnp.sum(before * onehot, axis=2).astype(jnp.int32)
    source = jnp.broadcast_to(jnp.arange(SOURCES, dtype=jnp.int32)[:, None], flat.shape)
    assign = jnp.broadcast_to(jnp.arange(TOK_NODE * TOPK, dtype=jnp.int32)[None, :], flat.shape)
    table = jnp.full((SOURCES, EXPERTS, CAP), -1, jnp.int32)
    table = table.at[source, flat, position].set(assign, mode="drop")
    return table


def block_sum(partials):
    rounded = partials.astype(jnp.bfloat16)
    rounded = lax.optimization_barrier(rounded)
    return jnp.sum(rounded.astype(jnp.float32), axis=0)


def expert_forward(rows, w_in, w_out):
    blocks = rows.astype(jnp.float32).reshape(SLOTS, N_LOCAL, D // N_LOCAL)
    w_blocks = w_in.astype(jnp.float32).reshape(N_LOCAL, D // N_LOCAL, 2, FF)
    pre = block_sum(jnp.einsum("rbd,bdgf->bfgr", blocks, w_blocks, precision=lax.Precision.HIGHEST))
    hidden = (jax.nn.silu(pre[:, 0]) * pre[:, 1]).astype(jnp.bfloat16)
    out = jnp.einsum("fr,fd->rd", hidden.astype(jnp.float32), w_out.astype(jnp.float32), precision=lax.Precision.HIGHEST)
    return out.astype(jnp.bfloat16)


def expert_backward(rows, saved, w_in, w_out):
    blocks = rows.astype(jnp.float32).reshape(SLOTS, N_LOCAL, D // N_LOCAL)
    w_blocks = w_out.astype(jnp.float32).reshape(FF, N_LOCAL, D // N_LOCAL)
    grad_hidden = block_sum(jnp.einsum("rbd,fbd->bfr", blocks, w_blocks, precision=lax.Precision.HIGHEST))
    gate_pre = saved[0].astype(jnp.float32)
    up_pre = saved[1].astype(jnp.float32)
    sigma = jax.nn.sigmoid(gate_pre)
    slope = sigma * (1.0 + gate_pre * (1.0 - sigma))
    d_pre = jnp.stack([grad_hidden * up_pre * slope, grad_hidden * gate_pre * sigma], axis=0).astype(jnp.bfloat16)
    out = jnp.einsum("gfr,dgf->rd", d_pre.astype(jnp.float32), w_in.astype(jnp.float32), precision=lax.Precision.HIGHEST)
    return out.astype(jnp.bfloat16)


def slot_tokens(table, expert):
    assign = table[:, expert, :]
    valid = assign >= 0
    safe = jnp.maximum(assign, 0)
    token = jnp.arange(SOURCES, dtype=jnp.int32)[:, None] * TOK_NODE + safe // TOPK
    return valid, safe, token


def layer_forward(inputs, ids, gates, w_in, w_out):
    table = slot_layout(ids)
    gate_flat = gates.reshape(SOURCES, TOK_NODE * TOPK)

    def one_expert(total, expert):
        valid, safe, token = slot_tokens(table, expert)
        rows = jnp.where(valid[..., None], inputs[token], jnp.zeros((), jnp.bfloat16)).reshape(SLOTS, D)
        out = expert_forward(rows, w_in[expert], w_out[expert])
        weight = jnp.where(valid, jnp.take_along_axis(gate_flat, safe, axis=1), 0.0).reshape(-1)
        total = total.at[token.reshape(-1)].add(out.astype(jnp.float32) * weight[:, None])
        return total, None

    total, _ = lax.scan(one_expert, jnp.zeros((TOKENS, D), jnp.float32), jnp.arange(EXPERTS, dtype=jnp.int32))
    return total.astype(jnp.bfloat16)


def layer_backward(grads, ids, gates, w_in, w_out, saved):
    table = slot_layout(ids)
    gate_flat = gates.reshape(SOURCES, TOK_NODE * TOPK)

    def one_expert(total, expert):
        valid, safe, token = slot_tokens(table, expert)
        gate = jnp.take_along_axis(gate_flat, safe, axis=1)
        scaled = (grads[token].astype(jnp.float32) * gate[..., None]).astype(jnp.bfloat16)
        rows = jnp.where(valid[..., None], scaled, jnp.zeros((), jnp.bfloat16)).reshape(SLOTS, D)
        out = expert_backward(rows, saved[expert], w_in[expert], w_out[expert])
        weight = jnp.where(valid, 1.0, 0.0).astype(jnp.float32).reshape(-1)
        total = total.at[token.reshape(-1)].add(out.astype(jnp.float32) * weight[:, None])
        return total, None

    total, _ = lax.scan(one_expert, jnp.zeros((TOKENS, D), jnp.float32), jnp.arange(EXPERTS, dtype=jnp.int32))
    return total.astype(jnp.bfloat16)


def reference(inputs_b, grads_a, experts_a, experts_b, gates_a, gates_b, w_gate_up, w_down, saved_a):
    def one_section(section):
        outputs = layer_forward(inputs_b[section], experts_b[section], gates_b[section], w_gate_up[section], w_down[section])
        input_grad = layer_backward(grads_a[section], experts_a[section], gates_a[section], w_gate_up[section], w_down[section], saved_a[section])
        return outputs, input_grad

    outputs_b, input_grads = lax.map(one_section, jnp.arange(SECTIONS, dtype=jnp.int32))
    grads_prev = jnp.concatenate([input_grads[1:], jnp.zeros_like(input_grads[:1])], axis=0)
    return outputs_b, grads_prev
```

```python
import functools

import jax
import jax.numpy as jnp
from jax import lax
from jax.experimental import pallas as pl
from jax.experimental.pallas import tpu as pltpu
from jax.sharding import PartitionSpec as P

BF = jnp.bfloat16
F32 = jnp.float32
VMEM_LIMIT = 48 * 1024 * 1024


def call(kernel, outs, args, flops=0, grid=None, in_specs=None, out_specs=None, scratch=()):
    moved = sum(a.size * a.dtype.itemsize for a in args)
    moved += sum(o.size * o.dtype.itemsize for o in jax.tree.leaves(outs))
    extra = {}
    if grid is not None:
        extra = dict(grid=grid, in_specs=in_specs, out_specs=out_specs)
    return pl.pallas_call(
        kernel,
        out_shape=outs,
        scratch_shapes=scratch,
        compiler_params=pltpu.CompilerParams(vmem_limit_bytes=VMEM_LIMIT),
        cost_estimate=pl.CostEstimate(flops=flops, bytes_accessed=moved, transcendentals=0),
        **extra,
    )(*args)


def shape(dims, dtype=BF):
    return jax.ShapeDtypeStruct(dims, dtype)


def dot(a, b, ca, cb):
    return lax.dot_general(a, b, (((ca,), (cb,)), ((), ())), preferred_element_type=F32)


def slot_table(ids_ref, gates_ref, experts, cap):
    top, tokens = ids_ref.shape
    expert = lax.broadcasted_iota(jnp.int32, (experts, tokens), 0)
    named = jnp.zeros((experts, tokens), F32)
    gate = jnp.zeros((experts, tokens), F32)
    for k in range(top):
        hit = (ids_ref[k : k + 1, :] == expert).astype(F32)
        named = named + hit
        gate = gate + hit * gates_ref[k : k + 1, :]
    earlier = lax.broadcasted_iota(jnp.int32, (tokens, tokens), 0) < lax.broadcasted_iota(
        jnp.int32, (tokens, tokens), 1
    )
    position = dot(named.astype(BF), earlier.astype(F32).astype(BF), 1, 0)
    position = jnp.where(named > 0, position, -1.0)
    slot = lax.broadcasted_iota(jnp.int32, (cap, tokens), 0).astype(F32)
    rows, gated = [], []
    for e in range(experts):
        fill = (position[e : e + 1, :] == slot).astype(F32)
        rows.append(fill)
        gated.append(fill * gate[e : e + 1, :])
    return jnp.concatenate(rows, axis=0), jnp.concatenate(gated, axis=0)


def dispatch_kernel(experts, cap, gate_rows, ids_ref, gates_ref, x_ref, out_ref):
    rows, gated = slot_table(ids_ref, gates_ref, experts, cap)
    picked = dot(rows.astype(BF), x_ref[...], 1, 0)
    if gate_rows:
        picked = picked * jnp.sum(gated, axis=1, keepdims=True)
    out_ref[...] = picked.astype(BF)


def combine_table_kernel(experts, cap, gate_rows, ids_ref, gates_ref, out_ref):
    rows, gated = slot_table(ids_ref, gates_ref, experts, cap)
    if gate_rows:
        out_ref[0] = rows.T.astype(BF)
    else:
        weight = gated.T
        high = weight.astype(BF)
        out_ref[0] = high
        out_ref[1] = (weight - high.astype(F32)).astype(BF)


def combine_kernel(table_ref, rows_ref, out_ref):
    total = dot(table_ref[0], rows_ref[...], 1, 0)
    for i in range(1, table_ref.shape[0]):
        total = total + dot(table_ref[i], rows_ref[...], 1, 0)
    out_ref[...] = total.astype(BF)


def up_kernel(x_ref, w_ref, out_ref):
    count = out_ref.shape[0]
    for j in range(count):
        w = jnp.concatenate([w_ref[0, :, 128 * j : 128 * j + 128], w_ref[1, :, 128 * j : 128 * j + 128]], axis=1)
        part = dot(x_ref[...], w, 1, 0).astype(BF)
        out_ref[j, 0] = part[:, :128]
        out_ref[j, 1] = part[:, 128:]


def activate_kernel(pre_ref, out_ref):
    gate = pre_ref[0].astype(F32)
    up = pre_ref[1].astype(F32)
    hidden = (gate / (1.0 + jnp.exp(-gate)) * up).astype(BF)
    if len(out_ref.shape) == 2:
        out_ref[...] = hidden
    else:
        for i in range(out_ref.shape[0]):
            out_ref[i] = hidden


def down_kernel(h_ref, w_ref, out_ref):
    blocks = h_ref.shape[0]
    h = jnp.concatenate([h_ref[i] for i in range(blocks)], axis=1)
    out_ref[...] = dot(h, w_ref[...], 1, 0).astype(BF)


def grad_hidden_kernel(x_ref, w_ref, out_ref):
    count = out_ref.shape[0]
    part = dot(x_ref[...], w_ref[...], 1, 1).astype(BF)
    for j in range(count):
        out_ref[j] = part[:, 128 * j : 128 * j + 128]


def slope_kernel(saved_ref, out_ref):
    gate = saved_ref[0].astype(F32)
    up = saved_ref[1].astype(F32)
    sigma = 1.0 / (1.0 + jnp.exp(-gate))
    out_ref[0] = (up * sigma * (1.0 + gate * (1.0 - sigma))).T
    out_ref[1] = (gate * sigma).T


def d_pre_kernel(parts_ref, slope_ref, out_ref):
    total = parts_ref[0].astype(F32)
    for i in range(1, parts_ref.shape[0]):
        total = total + parts_ref[i].astype(F32)
    out_ref[0] = (total * slope_ref[0]).astype(BF)
    out_ref[1] = (total * slope_ref[1]).astype(BF)


def input_grad_kernel(d_ref, w_ref, out_ref):
    blocks = d_ref.shape[0]
    d = jnp.concatenate([d_ref[i, g] for g in range(2) for i in range(blocks)], axis=1)
    w = jnp.concatenate([w_ref[0], w_ref[1]], axis=1)
    out_ref[...] = dot(d, w, 1, 1).astype(BF)


def shifted(value, axis, steps):
    count = lax.axis_size(axis)
    first, last = (max(0, -steps), min(count, count - steps))
    return lax.ppermute(value, axis, [(source, source + steps) for source in range(first, last)])


def exchange(value, axis):
    return lax.all_to_all(value, axis, split_axis=0, concat_axis=0, tiled=True)


def body(inputs_b, grads_a, experts_a, experts_b, gates_a, gates_b, w_gate_up, w_down, saved_a):
    nodes, locals_ = lax.axis_size("node"), lax.axis_size("local")
    tokens, width = inputs_b.shape[1:]
    slots = saved_a.shape[4]
    cap = slots // nodes
    units = saved_a.shape[3]
    ids_a, ids_b = experts_a[0].T, experts_b[0].T
    gate_a, gate_b = gates_a[0].T, gates_b[0].T
    w_out = w_down[0, 0]
    w_in = w_gate_up[0, 0].transpose(1, 0, 2)

    def dispatch(ids, gates, x, gate_rows):
        return call(
            functools.partial(dispatch_kernel, nodes, cap, gate_rows),
            shape((slots, width)),
            (ids, gates, x),
            flops=2 * slots * tokens * width,
        )

    def combine_table(ids, gates, gate_rows):
        return call(
            functools.partial(combine_table_kernel, nodes, cap, gate_rows),
            shape((1 if gate_rows else 2, tokens, slots)),
            (ids, gates),
            flops=10**6,
        )

    def combine(table, rows):
        return call(combine_kernel, shape((tokens, width)), (table, rows), flops=2 * tokens * slots * width)

    rows_a = exchange(dispatch(ids_a, gate_a, grads_a[0], True), "node")
    send_b = dispatch(ids_b, gate_b, inputs_b[0], False)
    slope = call(slope_kernel, shape((2, slots, units), F32), (saved_a[0, 0],), flops=10**6)
    table_a = combine_table(ids_a, gate_a, True)
    table_b = combine_table(ids_b, gate_b, False)
    part_a = call(
        grad_hidden_kernel,
        shape((locals_, slots, units)),
        (rows_a, w_out),
        flops=2 * slots * width * units * locals_,
    )
    send_b, part_a = lax.optimization_barrier((send_b, part_a))
    rows_b = exchange(send_b, "node")
    parts_a = exchange(part_a, "local")
    half = 2
    part_b = call(
        up_kernel,
        shape((locals_, 2, slots, units)),
        (rows_b, w_in),
        flops=4 * slots * width * units * locals_,
        grid=(locals_ // half,),
        in_specs=[
            pl.BlockSpec((slots, width), lambda i: (0, 0)),
            pl.BlockSpec((2, width, half * units), lambda i: (0, 0, i)),
        ],
        out_specs=pl.BlockSpec((half, 2, slots, units), lambda i: (i, 0, 0, 0)),
    )
    pre_b = lax.psum_scatter(
        part_b.reshape(locals_, 2 * slots, units), "local", scatter_dimension=0, tiled=True
    ).reshape(2, slots, units)
    d_pre = call(d_pre_kernel, shape((2, slots, units)), (parts_a, slope), flops=10**6)
    d_all = lax.all_gather(d_pre, "local", axis=0, tiled=True).reshape(locals_, 2, slots, units)
    hidden = call(activate_kernel, shape((locals_, slots, units)), (pre_b,), flops=10**6)
    hidden_all = exchange(hidden, "local")
    result_b = call(
        down_kernel, shape((slots, width)), (hidden_all, w_out), flops=2 * slots * width * units * locals_
    )
    result_a = call(
        input_grad_kernel, shape((slots, width)), (d_all, w_in), flops=4 * slots * width * units * locals_
    )
    returned_a = exchange(result_a, "node")
    input_grad = combine(table_a, returned_a)
    grads_prev = shifted(input_grad[None], "section", -1)
    returned_b = exchange(result_b, "node")
    outputs = combine(table_b, returned_b)
    return (outputs[None], grads_prev)


def solution(mesh):
    return jax.shard_map(
        body,
        mesh=mesh,
        in_specs=(
            P("section", "node", "local"),
            P("section", "node", "local"),
            P("section", "node", None),
            P("section", "node", None),
            P("section", "node", None),
            P("section", "node", None),
            P("section", "node", "local", None, None),
            P("section", "node", None, "local"),
            P("section", "node", None, "local", None),
        ),
        out_specs=(P("section", "node", "local"), P("section", "node", "local")),
        check_vma=False,
    )
```

```python
import functools

import jax
import jax.numpy as jnp
from jax import lax
from jax.experimental import pallas as pl
from jax.experimental.pallas import tpu as pltpu
from jax.sharding import PartitionSpec as P

BF = jnp.bfloat16
F32 = jnp.float32
VMEM_LIMIT = 48 * 1024 * 1024
LOCAL_ORDER = (3, 1, -3, -1, 4, 0, 2, -2)


def call(kernel, outs, args, flops=0, grid=None, in_specs=None, out_specs=None, scratch=(), scalars=False):
    moved = sum(a.size * a.dtype.itemsize for a in args)
    moved += sum(o.size * o.dtype.itemsize for o in jax.tree.leaves(outs))
    extra = {}
    if grid is not None:
        extra = dict(grid=grid, in_specs=in_specs, out_specs=out_specs)
    elif scalars:
        smem, vmem = pl.BlockSpec(memory_space=pltpu.SMEM), pl.BlockSpec(memory_space=pltpu.VMEM)
        extra = dict(in_specs=[smem] + [vmem] * (len(args) - 1))
    return pl.pallas_call(
        kernel,
        out_shape=outs,
        scratch_shapes=scratch,
        compiler_params=pltpu.CompilerParams(vmem_limit_bytes=VMEM_LIMIT),
        cost_estimate=pl.CostEstimate(flops=flops, bytes_accessed=moved, transcendentals=0),
        **extra,
    )(*args)


def shape(dims, dtype=BF):
    return jax.ShapeDtypeStruct(dims, dtype)


def dot(a, b, ca, cb):
    return lax.dot_general(a, b, (((ca,), (cb,)), ((), ())), preferred_element_type=F32)


def slot_table(ids_ref, gates_ref, experts, cap):
    top, tokens = ids_ref.shape
    expert = lax.broadcasted_iota(jnp.int32, (experts, tokens), 0)
    named = jnp.zeros((experts, tokens), F32)
    gate = jnp.zeros((experts, tokens), F32)
    for k in range(top):
        hit = (ids_ref[k : k + 1, :] == expert).astype(F32)
        named = named + hit
        gate = gate + hit * gates_ref[k : k + 1, :]
    earlier = lax.broadcasted_iota(jnp.int32, (tokens, tokens), 0) < lax.broadcasted_iota(
        jnp.int32, (tokens, tokens), 1
    )
    position = dot(named.astype(BF), earlier.astype(F32).astype(BF), 1, 0)
    position = jnp.where(named > 0, position, -1.0)
    slot = lax.broadcasted_iota(jnp.int32, (cap, tokens), 0).astype(F32)
    rows, gated = [], []
    for e in range(experts):
        fill = (position[e : e + 1, :] == slot).astype(F32)
        rows.append(fill)
        gated.append(fill * gate[e : e + 1, :])
    return jnp.concatenate(rows, axis=0), jnp.concatenate(gated, axis=0)


def dispatch_kernel(experts, cap, gate_rows, ids_ref, gates_ref, x_ref, out_ref):
    rows, gated = slot_table(ids_ref, gates_ref, experts, cap)
    picked = dot(rows.astype(BF), x_ref[...], 1, 0)
    if gate_rows:
        picked = picked * jnp.sum(gated, axis=1, keepdims=True)
    out_ref[...] = picked.astype(BF)


def combine_table_kernel(experts, cap, gate_rows, ids_ref, gates_ref, out_ref):
    rows, gated = slot_table(ids_ref, gates_ref, experts, cap)
    if gate_rows:
        out_ref[0] = rows.T.astype(BF)
    else:
        weight = gated.T
        high = weight.astype(BF)
        out_ref[0] = high
        out_ref[1] = (weight - high.astype(F32)).astype(BF)


def combine_kernel(table_ref, rows_ref, out_ref):
    total = dot(table_ref[0], rows_ref[...], 1, 0)
    for i in range(1, table_ref.shape[0]):
        total = total + dot(table_ref[i], rows_ref[...], 1, 0)
    out_ref[...] = total.astype(BF)


def spread_refs(ahead_ref, behind_ref, across_ref, own_ref):
    return [ahead_ref.at[0], ahead_ref.at[1], behind_ref.at[0], behind_ref.at[1], across_ref, *[own_ref.at[i] for i in range(3)]]


def up_kernel(x_ref, w_ref, out_ref):
    count = out_ref.shape[0]
    for j in range(count):
        w = jnp.concatenate([w_ref[0, :, 128 * j : 128 * j + 128], w_ref[1, :, 128 * j : 128 * j + 128]], axis=1)
        part = dot(x_ref[...], w, 1, 0).astype(BF)
        out_ref[j, 0] = part[:, :128]
        out_ref[j, 1] = part[:, 128:]


def grad_hidden_kernel(place_ref, x_ref, w_ref, *out_refs):
    outs = spread_refs(*out_refs)
    unit = outs[0].shape[-1]
    for i in range(0, len(outs), 2):
        w = jnp.concatenate(
            [w_ref[pl.ds(pl.multiple_of(place_ref[i + j] * unit, unit), unit), :] for j in range(2)], axis=0
        )
        part = dot(x_ref[...], w, 1, 1).astype(BF)
        outs[i][...] = part[:, :unit]
        outs[i + 1][...] = part[:, unit:]


def relay_sum_kernel(core_ref, own_ref, ahead_ref, behind_ref, across_ref, plus_ref, minus_ref):
    plus = own_ref[1].astype(F32) + ahead_ref[0].astype(F32)
    minus = own_ref[2].astype(F32) + behind_ref[0].astype(F32)
    across = across_ref[...].astype(F32)
    first = core_ref[0] == 0
    zero = jnp.zeros_like(across)
    plus_ref[...] = (plus + jnp.where(first, zero, across)).astype(BF)
    minus_ref[...] = (minus + jnp.where(first, across, zero)).astype(BF)


def arrived_sum(own_ref, ahead_ref, behind_ref, plus_ref, minus_ref):
    total = own_ref[0].astype(F32)
    for part in (ahead_ref[1], behind_ref[1], plus_ref[...], minus_ref[...]):
        total = total + part.astype(F32)
    return total


def activate_kernel(pre_ref, out_ref):
    gate, up = pre_ref[0].astype(F32), pre_ref[1].astype(F32)
    out_ref[...] = (gate / (1.0 + jnp.exp(-gate)) * up).astype(BF)


def grad_sum_kernel(*refs):
    refs[-1][...] = arrived_sum(*refs[:-1]).astype(BF)


def pack_kernel(core_ref, own_ref, low_ref, high_ref, ahead_ref, behind_ref, across_ref):
    ahead_ref[0] = own_ref[...]
    ahead_ref[1] = low_ref[...]
    behind_ref[0] = own_ref[...]
    behind_ref[1] = high_ref[...]
    across_ref[...] = jnp.where(core_ref[0] == 0, low_ref[...], high_ref[...])


def down_kernel(h_ref, w_ref, out_ref):
    blocks = h_ref.shape[0]
    h = jnp.concatenate([h_ref[i] for i in range(blocks)], axis=1)
    out_ref[...] = dot(h, w_ref[...], 1, 0).astype(BF)


def input_grad_kernel(
    place_ref, own_ref, low_ref, high_ref, ahead_ref, behind_ref, across_ref, slope_ref, w_ref, out_ref
):
    blocks = [ahead_ref.at[1], ahead_ref.at[0], behind_ref.at[1], behind_ref.at[0], across_ref, own_ref, high_ref, low_ref]
    source = [2, 3, 0, 1, 4, 5, 6, 7]
    unit = own_ref.shape[-1]
    total = None
    for block, i in zip(blocks, source):
        at = place_ref[i]
        columns = pl.ds(pl.multiple_of(at * unit, unit), unit)
        w = jnp.concatenate([w_ref[0, :, columns], w_ref[1, :, columns]], axis=1)
        h = block[...].astype(F32)
        d = jnp.concatenate([(h * slope_ref[at, g].astype(F32)).astype(BF) for g in range(2)], axis=1)
        part = dot(d, w, 1, 1)
        total = part if total is None else total + part
    out_ref[...] = total.astype(BF)


def rotated(value, steps, mirrored=False):
    nodes, count = lax.axis_size("node"), lax.axis_size("local")
    pairs = []
    for node in range(nodes):
        way = -steps if mirrored and node % 2 else steps
        pairs += [(node * count + i, node * count + (i + way) % count) for i in range(count)]
    return lax.ppermute(value, ("node", "local"), pairs)


def slope_kernel(saved_ref, out_ref):
    gate = saved_ref[0].astype(F32)
    up = saved_ref[1].astype(F32)
    sigma = 1.0 / (1.0 + jnp.exp(-gate))
    out_ref[0] = (up * sigma * (1.0 + gate * (1.0 - sigma))).T.astype(BF)
    out_ref[1] = (gate * sigma).T.astype(BF)


def shifted(value, axis, steps):
    count = lax.axis_size(axis)
    first, last = (max(0, -steps), min(count, count - steps))
    return lax.ppermute(value, axis, [(source, source + steps) for source in range(first, last)])


def rotated(value, steps, mirrored=False):
    nodes, count = lax.axis_size("node"), lax.axis_size("local")
    pairs = []
    for node in range(nodes):
        way = -steps if mirrored and node % 2 else steps
        pairs += [(node * count + i, node * count + (i + way) % count) for i in range(count)]
    return lax.ppermute(value, ("node", "local"), pairs)


def shifted(value, axis, steps):
    count = lax.axis_size(axis)
    first, last = (max(0, -steps), min(count, count - steps))
    return lax.ppermute(value, axis, [(source, source + steps) for source in range(first, last)])


def exchange(value, axis):
    return lax.all_to_all(value, axis, split_axis=0, concat_axis=0, tiled=True)


def body(inputs_b, grads_a, experts_a, experts_b, gates_a, gates_b, w_gate_up, w_down, saved_a):
    nodes, locals_ = lax.axis_size("node"), lax.axis_size("local")
    tokens, width = inputs_b.shape[1:]
    slots = saved_a.shape[4]
    cap = slots // nodes
    units = saved_a.shape[3]
    ids_a, ids_b = experts_a[0].T, experts_b[0].T
    gate_a, gate_b = gates_a[0].T, gates_b[0].T
    w_out = w_down[0, 0]
    w_in = w_gate_up[0, 0].transpose(1, 0, 2)

    def dispatch(ids, gates, x, gate_rows):
        return call(
            functools.partial(dispatch_kernel, nodes, cap, gate_rows),
            shape((slots, width)),
            (ids, gates, x),
            flops=2 * slots * tokens * width,
        )

    def combine_table(ids, gates, gate_rows):
        return call(
            functools.partial(combine_table_kernel, nodes, cap, gate_rows),
            shape((1 if gate_rows else 2, tokens, slots)),
            (ids, gates),
            flops=10**6,
        )

    def combine(table, rows):
        return call(combine_kernel, shape((tokens, width)), (table, rows), flops=2 * tokens * slots * width)

    me = lax.axis_index("local").astype(jnp.int32)
    core = (lax.axis_index("node") % 2).astype(jnp.int32).reshape(1)
    place = (me + jnp.array(LOCAL_ORDER, jnp.int32)) % locals_

    def partials(kernel, block, x, w):
        kinds = [shape(lead + block) for lead in ((2,), (2,), (), (3,))]
        flops = 2 * width * locals_ * functools.reduce(lambda a, b: a * b, block)
        return call(kernel, kinds, (place, x, w), flops=flops, scalars=True)

    def relay_sum(own, ahead, behind, across):
        kind = shape(across.shape)
        return call(relay_sum_kernel, (kind, kind), (core, own, ahead, behind, across), flops=10**6, scalars=True)

    def gather_local(own):
        low, high = rotated(own, 2), rotated(own, -2)
        two, one = shape((2,) + own.shape), shape(own.shape)
        ahead, behind, across = call(pack_kernel, (two, two, one), (core, own, low, high), scalars=True)
        across = rotated(across, 2, True)
        return own, low, high, rotated(ahead, 1), rotated(behind, -1), across

    send_a = dispatch(ids_a, gate_a, grads_a[0], True)
    rows_a = exchange(send_a, "node")
    send_b = dispatch(ids_b, gate_b, inputs_b[0], False)
    slope = call(slope_kernel, shape((2, slots, units)), (saved_a[0, 0],), flops=10**6)
    table_a = combine_table(ids_a, gate_a, True)
    table_b = combine_table(ids_b, gate_b, False)
    slopes = lax.all_gather(slope, "local", axis=0, tiled=True).reshape(locals_, 2, slots, units)
    rows_a, send_b, w_in, table_a, table_b = lax.optimization_barrier((rows_a, send_b, w_in, table_a, table_b))
    rows_b = exchange(send_b, "node")
    ahead, behind, across, own = partials(grad_hidden_kernel, (slots, units), rows_a, w_out)
    across = rotated(across, -2, True)
    ahead = rotated(ahead, 1)
    behind = rotated(behind, -1)
    half = 2
    part_b = call(
        up_kernel,
        shape((locals_, 2, slots, units)),
        (rows_b, w_in),
        flops=4 * slots * width * units * locals_,
        grid=(locals_ // half,),
        in_specs=[
            pl.BlockSpec((slots, width), lambda i: (0, 0)),
            pl.BlockSpec((2, width, half * units), lambda i: (0, 0, i)),
        ],
        out_specs=pl.BlockSpec((half, 2, slots, units), lambda i: (i, 0, 0, 0)),
    )
    ahead, behind, across, part_b, slopes = lax.optimization_barrier((ahead, behind, across, part_b, slopes))
    plus, minus = relay_sum(own, ahead, behind, across)
    pre_b = lax.psum_scatter(
        part_b.reshape(locals_, 2 * slots, units), "local", scatter_dimension=0, tiled=True
    ).reshape(2, slots, units)
    sums_a = (own, ahead, behind, rotated(plus, 2), rotated(minus, -2))
    grad_hidden = call(grad_sum_kernel, shape((slots, units)), sums_a, flops=10**6)
    grad_hidden = gather_local(grad_hidden)
    pre_b, _, _, _ = lax.optimization_barrier((pre_b, *grad_hidden[3:]))
    result_a = call(
        input_grad_kernel,
        shape((slots, width)),
        (place, *grad_hidden, slopes, w_in),
        flops=4 * slots * width * units * locals_,
        scalars=True,
    )
    hidden = call(activate_kernel, shape((slots, units)), (pre_b,), flops=10**6)
    hidden_all = lax.all_gather(hidden, "local", axis=0, tiled=True).reshape(locals_, slots, units)
    result_b = call(
        down_kernel, shape((slots, width)), (hidden_all, w_out), flops=2 * slots * width * units * locals_
    )
    returned_a = exchange(result_a, "node")
    returned_a, result_b = lax.optimization_barrier((returned_a, result_b))
    returned_b = exchange(result_b, "node")
    input_grad = combine(table_a, returned_a)
    grads_prev = shifted(input_grad[None], "section", -1)
    outputs = combine(table_b, returned_b)
    return (outputs[None], grads_prev)


def solution(mesh):
    return jax.shard_map(
        body,
        mesh=mesh,
        in_specs=(
            P("section", "node", "local"),
            P("section", "node", "local"),
            P("section", "node", None),
            P("section", "node", None),
            P("section", "node", None),
            P("section", "node", None),
            P("section", "node", "local", None, None),
            P("section", "node", None, "local"),
            P("section", "node", None, "local", None),
        ),
        out_specs=(P("section", "node", "local"), P("section", "node", "local")),
        check_vma=False,
    )
```

```python
import functools

import jax
import jax.numpy as jnp
from jax import lax
from jax.experimental import pallas as pl
from jax.experimental.pallas import tpu as pltpu
from jax.sharding import PartitionSpec as P

BF = jnp.bfloat16
F32 = jnp.float32
VMEM_LIMIT = 48 * 1024 * 1024
LOCAL_ORDER = (3, 1, -3, -1, 4, 0, 2, -2)


def call(kernel, outs, args, flops=0, in_specs=None, out_specs=None, scratch=(), scalars=False):
    moved = sum(a.size * a.dtype.itemsize for a in args)
    moved += sum(o.size * o.dtype.itemsize for o in jax.tree.leaves(outs))
    extra = {}
    if in_specs is not None:
        extra = dict(in_specs=in_specs, out_specs=out_specs)
    elif scalars:
        smem, vmem = pl.BlockSpec(memory_space=pltpu.SMEM), pl.BlockSpec(memory_space=pltpu.VMEM)
        extra = dict(in_specs=[smem] + [vmem] * (len(args) - 1))
    return pl.pallas_call(
        kernel,
        out_shape=outs,
        scratch_shapes=scratch,
        compiler_params=pltpu.CompilerParams(vmem_limit_bytes=VMEM_LIMIT),
        cost_estimate=pl.CostEstimate(flops=flops, bytes_accessed=moved, transcendentals=0),
        **extra,
    )(*args)


def shape(dims, dtype=BF):
    return jax.ShapeDtypeStruct(dims, dtype)


def dot(a, b, ca, cb):
    return lax.dot_general(a, b, (((ca,), (cb,)), ((), ())), preferred_element_type=F32)


def slot_table(ids_ref, gates_ref, experts, cap):
    top, tokens = ids_ref.shape
    expert = lax.broadcasted_iota(jnp.int32, (experts, tokens), 0)
    named = jnp.zeros((experts, tokens), F32)
    gate = jnp.zeros((experts, tokens), F32)
    for k in range(top):
        hit = (ids_ref[k : k + 1, :] == expert).astype(F32)
        named = named + hit
        gate = gate + hit * gates_ref[k : k + 1, :]
    earlier = lax.broadcasted_iota(jnp.int32, (tokens, tokens), 0) < lax.broadcasted_iota(
        jnp.int32, (tokens, tokens), 1
    )
    position = dot(named.astype(BF), earlier.astype(F32).astype(BF), 1, 0)
    position = jnp.where(named > 0, position, -1.0)
    slot = lax.broadcasted_iota(jnp.int32, (cap, tokens), 0).astype(F32)
    rows, gated = [], []
    for e in range(experts):
        fill = (position[e : e + 1, :] == slot).astype(F32)
        rows.append(fill)
        gated.append(fill * gate[e : e + 1, :])
    return jnp.concatenate(rows, axis=0), jnp.concatenate(gated, axis=0)


def dispatch_kernel(experts, cap, gate_rows, ids_from, gates_from, x_from, out_ref, ids_ref, gates_ref, x_ref, sems):
    copies = [
        pltpu.make_async_copy(source, target, sems.at[i])
        for i, (source, target) in enumerate([(ids_from, ids_ref), (gates_from, gates_ref), (x_from, x_ref)])
    ]
    for copy in copies:
        copy.start()
    for copy in copies:
        copy.wait()
    rows, gated = slot_table(ids_ref, gates_ref, experts, cap)
    picked = dot(rows.astype(BF), x_ref[...], 1, 0)
    if gate_rows:
        picked = picked * jnp.sum(gated, axis=1, keepdims=True)
    out_ref[...] = picked.astype(BF)


def combine_table_kernel(experts, cap, gate_rows, ids_ref, gates_ref, out_ref):
    rows, gated = slot_table(ids_ref, gates_ref, experts, cap)
    if gate_rows:
        out_ref[0] = rows.T.astype(BF)
    else:
        weight = gated.T
        high = weight.astype(BF)
        out_ref[0] = high
        out_ref[1] = (weight - high.astype(F32)).astype(BF)


def combine_kernel(table_ref, rows_ref, out_ref):
    total = dot(table_ref[0], rows_ref[...], 1, 0)
    for i in range(1, table_ref.shape[0]):
        total = total + dot(table_ref[i], rows_ref[...], 1, 0)
    out_ref[...] = total.astype(BF)


def spread_refs(ahead_ref, behind_ref, across_ref, own_ref):
    return [ahead_ref.at[0], ahead_ref.at[1], behind_ref.at[0], behind_ref.at[1], across_ref, *[own_ref.at[i] for i in range(3)]]


def up_kernel(x_ref, w_ref, out_ref, held, sems):
    count, unit = held.shape[0], held.shape[-1]
    copies = []
    for j in range(count):
        w = jnp.concatenate([w_ref[g, :, unit * j : unit * (j + 1)] for g in range(2)], axis=1)
        part = dot(x_ref[...], w, 1, 0).astype(BF)
        held[j, 0] = part[:, :unit]
        held[j, 1] = part[:, unit:]
        copy = pltpu.make_async_copy(held.at[j], out_ref.at[j], sems.at[j])
        copy.start()
        copies.append(copy)
    for copy in copies:
        copy.wait()


def grad_hidden_kernel(place_ref, x_ref, w_ref, *out_refs):
    outs = spread_refs(*out_refs)
    unit = outs[0].shape[-1]
    for i in range(0, len(outs), 2):
        w = jnp.concatenate(
            [w_ref[pl.ds(pl.multiple_of(place_ref[i + j] * unit, unit), unit), :] for j in range(2)], axis=0
        )
        part = dot(x_ref[...], w, 1, 1).astype(BF)
        outs[i][...] = part[:, :unit]
        outs[i + 1][...] = part[:, unit:]


def relay_sum_kernel(core_ref, own_ref, ahead_ref, behind_ref, across_ref, plus_ref, minus_ref):
    plus = own_ref[1].astype(F32) + ahead_ref[0].astype(F32)
    minus = own_ref[2].astype(F32) + behind_ref[0].astype(F32)
    across = across_ref[...].astype(F32)
    first = core_ref[0] == 0
    zero = jnp.zeros_like(across)
    plus_ref[...] = (plus + jnp.where(first, zero, across)).astype(BF)
    minus_ref[...] = (minus + jnp.where(first, across, zero)).astype(BF)


def arrived_sum(own_ref, ahead_ref, behind_ref, plus_ref, minus_ref):
    total = own_ref[0].astype(F32)
    for part in (ahead_ref[1], behind_ref[1], plus_ref[...], minus_ref[...]):
        total = total + part.astype(F32)
    return total


def activate_kernel(pre_ref, out_ref):
    gate, up = pre_ref[0].astype(F32), pre_ref[1].astype(F32)
    out_ref[...] = (gate / (1.0 + jnp.exp(-gate)) * up).astype(BF)


def grad_sum_kernel(*refs):
    refs[-1][...] = arrived_sum(*refs[:-1]).astype(BF)


def pack_kernel(core_ref, own_ref, low_ref, high_ref, ahead_ref, behind_ref, across_ref):
    ahead_ref[0] = own_ref[...]
    ahead_ref[1] = low_ref[...]
    behind_ref[0] = own_ref[...]
    behind_ref[1] = high_ref[...]
    across_ref[...] = jnp.where(core_ref[0] == 0, low_ref[...], high_ref[...])


def down_kernel(h_ref, w_ref, out_ref):
    blocks = h_ref.shape[0]
    h = jnp.concatenate([h_ref[i] for i in range(blocks)], axis=1)
    out_ref[...] = dot(h, w_ref[...], 1, 0).astype(BF)


def input_grad_kernel(
    place_ref, own_ref, low_ref, high_ref, ahead_ref, behind_ref, across_ref, slope_ref, w_ref, out_ref
):
    blocks = [ahead_ref.at[1], ahead_ref.at[0], behind_ref.at[1], behind_ref.at[0], across_ref, own_ref, high_ref, low_ref]
    source = [2, 3, 0, 1, 4, 5, 6, 7]
    unit = own_ref.shape[-1]
    total = None
    for block, i in zip(blocks, source):
        at = place_ref[i]
        columns = pl.ds(pl.multiple_of(at * unit, unit), unit)
        w = jnp.concatenate([w_ref[0, :, columns], w_ref[1, :, columns]], axis=1)
        h = block[...].astype(F32)
        d = jnp.concatenate([(h * slope_ref[at, g].astype(F32)).astype(BF) for g in range(2)], axis=1)
        part = dot(d, w, 1, 1)
        total = part if total is None else total + part
    out_ref[...] = total.astype(BF)


def rotated(value, steps, mirrored=False):
    nodes, count = lax.axis_size("node"), lax.axis_size("local")
    pairs = []
    for node in range(nodes):
        way = -steps if mirrored and node % 2 else steps
        pairs += [(node * count + i, node * count + (i + way) % count) for i in range(count)]
    return lax.ppermute(value, ("node", "local"), pairs)


def slope_kernel(saved_ref, out_ref):
    gate = saved_ref[0].astype(F32)
    up = saved_ref[1].astype(F32)
    sigma = 1.0 / (1.0 + jnp.exp(-gate))
    out_ref[0] = (up * sigma * (1.0 + gate * (1.0 - sigma))).T.astype(BF)
    out_ref[1] = (gate * sigma).T.astype(BF)


def shifted(value, axis, steps):
    count = lax.axis_size(axis)
    first, last = (max(0, -steps), min(count, count - steps))
    return lax.ppermute(value, axis, [(source, source + steps) for source in range(first, last)])


def rotated(value, steps, mirrored=False):
    nodes, count = lax.axis_size("node"), lax.axis_size("local")
    pairs = []
    for node in range(nodes):
        way = -steps if mirrored and node % 2 else steps
        pairs += [(node * count + i, node * count + (i + way) % count) for i in range(count)]
    return lax.ppermute(value, ("node", "local"), pairs)


def shifted(value, axis, steps):
    count = lax.axis_size(axis)
    first, last = (max(0, -steps), min(count, count - steps))
    return lax.ppermute(value, axis, [(source, source + steps) for source in range(first, last)])


def exchange(value, axis):
    return lax.all_to_all(value, axis, split_axis=0, concat_axis=0, tiled=True)


def body(inputs_b, grads_a, experts_a, experts_b, gates_a, gates_b, w_gate_up, w_down, saved_a):
    nodes, locals_ = lax.axis_size("node"), lax.axis_size("local")
    tokens, width = inputs_b.shape[1:]
    slots = saved_a.shape[4]
    cap = slots // nodes
    units = saved_a.shape[3]
    ids_a, ids_b = experts_a[0].T, experts_b[0].T
    gate_a, gate_b = gates_a[0].T, gates_b[0].T
    w_out = w_down[0, 0]
    w_in = w_gate_up[0, 0].transpose(1, 0, 2)

    def dispatch(ids, gates, x, gate_rows):
        return call(
            functools.partial(dispatch_kernel, nodes, cap, gate_rows),
            shape((slots, width)),
            (ids, gates, x),
            flops=2 * slots * tokens * width,
            in_specs=[pl.BlockSpec(memory_space=pl.ANY)] * 3,
            out_specs=pl.BlockSpec(memory_space=pltpu.VMEM),
            scratch=[pltpu.VMEM(a.shape, a.dtype) for a in (ids, gates, x)] + [pltpu.SemaphoreType.DMA((3,))],
        )

    def combine_table(ids, gates, gate_rows):
        return call(
            functools.partial(combine_table_kernel, nodes, cap, gate_rows),
            shape((1 if gate_rows else 2, tokens, slots)),
            (ids, gates),
            flops=10**6,
        )

    def combine(table, rows):
        return call(combine_kernel, shape((tokens, width)), (table, rows), flops=2 * tokens * slots * width)

    me = lax.axis_index("local").astype(jnp.int32)
    core = (lax.axis_index("node") % 2).astype(jnp.int32).reshape(1)
    place = (me + jnp.array(LOCAL_ORDER, jnp.int32)) % locals_

    def partials(kernel, block, x, w):
        kinds = [shape(lead + block) for lead in ((2,), (2,), (), (3,))]
        flops = 2 * width * locals_ * functools.reduce(lambda a, b: a * b, block)
        return call(kernel, kinds, (place, x, w), flops=flops, scalars=True)

    def relay_sum(own, ahead, behind, across):
        kind = shape(across.shape)
        return call(relay_sum_kernel, (kind, kind), (core, own, ahead, behind, across), flops=10**6, scalars=True)

    def gather_local(own):
        low, high = rotated(own, 2), rotated(own, -2)
        two, one = shape((2,) + own.shape), shape(own.shape)
        ahead, behind, across = call(pack_kernel, (two, two, one), (core, own, low, high), scalars=True)
        across = rotated(across, 2, True)
        return own, low, high, rotated(ahead, 1), rotated(behind, -1), across

    send_a = dispatch(ids_a, gate_a, grads_a[0], True)
    rows_a = exchange(send_a, "node")
    send_b = dispatch(ids_b, gate_b, inputs_b[0], False)
    send_a, saved = lax.optimization_barrier((send_a, saved_a))
    slope = call(slope_kernel, shape((2, slots, units)), (saved[0, 0],), flops=10**6)
    table_a = combine_table(ids_a, gate_a, True)
    table_b = combine_table(ids_b, gate_b, False)
    slopes = lax.all_gather(slope, "local", axis=0, tiled=True).reshape(locals_, 2, slots, units)
    rows_a, send_b, w_in, table_a, table_b = lax.optimization_barrier((rows_a, send_b, w_in, table_a, table_b))
    rows_b = exchange(send_b, "node")
    ahead, behind, across, own = partials(grad_hidden_kernel, (slots, units), rows_a, w_out)
    across = rotated(across, -2, True)
    ahead = rotated(ahead, 1)
    behind = rotated(behind, -1)
    spec = pl.BlockSpec(memory_space=pltpu.VMEM)
    part_b = call(
        up_kernel,
        shape((locals_, 2, slots, units)),
        (rows_b, w_in),
        flops=4 * slots * width * units * locals_,
        in_specs=[spec, spec],
        out_specs=pl.BlockSpec(memory_space=pltpu.HBM),
        scratch=[pltpu.VMEM((locals_, 2, slots, units), BF), pltpu.SemaphoreType.DMA((locals_,))],
    )
    ahead, behind, across, part_b, slopes = lax.optimization_barrier((ahead, behind, across, part_b, slopes))
    plus, minus = relay_sum(own, ahead, behind, across)
    pre_b = lax.psum_scatter(
        part_b.reshape(locals_, 2 * slots, units), "local", scatter_dimension=0, tiled=True
    ).reshape(2, slots, units)
    sums_a = (own, ahead, behind, rotated(plus, 2), rotated(minus, -2))
    grad_hidden = call(grad_sum_kernel, shape((slots, units)), sums_a, flops=10**6)
    grad_hidden = gather_local(grad_hidden)
    pre_b, _, _, _ = lax.optimization_barrier((pre_b, *grad_hidden[3:]))
    result_a = call(
        input_grad_kernel,
        shape((slots, width)),
        (place, *grad_hidden, slopes, w_in),
        flops=4 * slots * width * units * locals_,
        scalars=True,
    )
    hidden = call(activate_kernel, shape((slots, units)), (pre_b,), flops=10**6)
    hidden_all = lax.all_gather(hidden, "local", axis=0, tiled=True).reshape(locals_, slots, units)
    result_b = call(
        down_kernel, shape((slots, width)), (hidden_all, w_out), flops=2 * slots * width * units * locals_
    )
    returned_a = exchange(result_a, "node")
    returned_a, result_b = lax.optimization_barrier((returned_a, result_b))
    returned_b = exchange(result_b, "node")
    input_grad = combine(table_a, returned_a)
    grads_prev = shifted(input_grad[None], "section", -1)
    outputs = combine(table_b, returned_b)
    return (outputs[None], grads_prev)


def solution(mesh):
    return jax.shard_map(
        body,
        mesh=mesh,
        in_specs=(
            P("section", "node", "local"),
            P("section", "node", "local"),
            P("section", "node", None),
            P("section", "node", None),
            P("section", "node", None),
            P("section", "node", None),
            P("section", "node", "local", None, None),
            P("section", "node", None, "local"),
            P("section", "node", None, "local", None),
        ),
        out_specs=(P("section", "node", "local"), P("section", "node", "local")),
        check_vma=False,
    )
```

```python
import functools

import jax
import jax.numpy as jnp
from jax import lax
from jax.experimental import pallas as pl
from jax.experimental.pallas import tpu as pltpu
from jax.sharding import PartitionSpec as P

BF = jnp.bfloat16
F32 = jnp.float32
VMEM_LIMIT = 48 * 1024 * 1024
VMEM_WHOLE = 60 * 1024 * 1024
LOCAL_ORDER = (3, 1, -3, -1, 4, 0, 2, -2)


def call(kernel, outs, args, flops=0, grid=None, in_specs=None, out_specs=None, scratch=(), scalars=False, limit=VMEM_LIMIT):
    moved = sum(a.size * a.dtype.itemsize for a in args)
    moved += sum(o.size * o.dtype.itemsize for o in jax.tree.leaves(outs))
    extra = {}
    if grid is not None:
        extra = dict(grid=grid, in_specs=in_specs, out_specs=out_specs)
    elif scalars:
        smem, vmem = pl.BlockSpec(memory_space=pltpu.SMEM), pl.BlockSpec(memory_space=pltpu.VMEM)
        extra = dict(in_specs=[smem] + [vmem] * (len(args) - 1))
    return pl.pallas_call(
        kernel,
        out_shape=outs,
        scratch_shapes=scratch,
        compiler_params=pltpu.CompilerParams(vmem_limit_bytes=limit),
        cost_estimate=pl.CostEstimate(flops=flops, bytes_accessed=moved, transcendentals=0),
        **extra,
    )(*args)


def shape(dims, dtype=BF):
    return jax.ShapeDtypeStruct(dims, dtype)


def dot(a, b, ca, cb):
    return lax.dot_general(a, b, (((ca,), (cb,)), ((), ())), preferred_element_type=F32)


def slot_table(ids_ref, gates_ref, experts, cap):
    top, tokens = ids_ref.shape
    expert = lax.broadcasted_iota(jnp.int32, (experts, tokens), 0)
    named = jnp.zeros((experts, tokens), F32)
    gate = jnp.zeros((experts, tokens), F32)
    for k in range(top):
        hit = (ids_ref[k : k + 1, :] == expert).astype(F32)
        named = named + hit
        gate = gate + hit * gates_ref[k : k + 1, :]
    earlier = lax.broadcasted_iota(jnp.int32, (tokens, tokens), 0) < lax.broadcasted_iota(
        jnp.int32, (tokens, tokens), 1
    )
    position = dot(named.astype(BF), earlier.astype(F32).astype(BF), 1, 0)
    position = jnp.where(named > 0, position, -1.0)
    slot = lax.broadcasted_iota(jnp.int32, (cap, tokens), 0).astype(F32)
    rows, gated = [], []
    for e in range(experts):
        fill = (position[e : e + 1, :] == slot).astype(F32)
        rows.append(fill)
        gated.append(fill * gate[e : e + 1, :])
    return jnp.concatenate(rows, axis=0), jnp.concatenate(gated, axis=0)


def dispatch_kernel(experts, cap, gate_rows, ids_ref, gates_ref, x_ref, out_ref):
    rows, gated = slot_table(ids_ref, gates_ref, experts, cap)
    picked = dot(rows.astype(BF), x_ref[...], 1, 0)
    if gate_rows:
        picked = picked * jnp.sum(gated, axis=1, keepdims=True)
    out_ref[...] = picked.astype(BF)


def combine_table_kernel(experts, cap, gate_rows, ids_ref, gates_ref, out_ref):
    rows, gated = slot_table(ids_ref, gates_ref, experts, cap)
    if gate_rows:
        out_ref[0] = rows.T.astype(BF)
    else:
        weight = gated.T
        high = weight.astype(BF)
        out_ref[0] = high
        out_ref[1] = (weight - high.astype(F32)).astype(BF)


def combine_kernel(table_ref, rows_ref, out_ref):
    total = dot(table_ref[0], rows_ref[...], 1, 0)
    for i in range(1, table_ref.shape[0]):
        total = total + dot(table_ref[i], rows_ref[...], 1, 0)
    out_ref[...] = total.astype(BF)


def spread_refs(ahead_ref, behind_ref, across_ref, own_ref):
    return [ahead_ref.at[0], ahead_ref.at[1], behind_ref.at[0], behind_ref.at[1], across_ref, *[own_ref.at[i] for i in range(3)]]


def up_kernel(x_ref, w_ref, out_ref):
    count = out_ref.shape[0]
    for j in range(count):
        w = jnp.concatenate([w_ref[0, :, 128 * j : 128 * j + 128], w_ref[1, :, 128 * j : 128 * j + 128]], axis=1)
        part = dot(x_ref[...], w, 1, 0).astype(BF)
        out_ref[j, 0] = part[:, :128]
        out_ref[j, 1] = part[:, 128:]


def grad_hidden_kernel(place_ref, x_ref, w_ref, *out_refs):
    outs = spread_refs(*out_refs)
    unit = outs[0].shape[-1]
    for i in range(0, len(outs), 2):
        w = jnp.concatenate(
            [w_ref[pl.ds(pl.multiple_of(place_ref[i + j] * unit, unit), unit), :] for j in range(2)], axis=0
        )
        part = dot(x_ref[...], w, 1, 1).astype(BF)
        outs[i][...] = part[:, :unit]
        outs[i + 1][...] = part[:, unit:]


def relay_sum_kernel(core_ref, own_ref, ahead_ref, behind_ref, across_ref, plus_ref, minus_ref):
    plus = own_ref[1].astype(F32) + ahead_ref[0].astype(F32)
    minus = own_ref[2].astype(F32) + behind_ref[0].astype(F32)
    across = across_ref[...].astype(F32)
    first = core_ref[0] == 0
    zero = jnp.zeros_like(across)
    plus_ref[...] = (plus + jnp.where(first, zero, across)).astype(BF)
    minus_ref[...] = (minus + jnp.where(first, across, zero)).astype(BF)


def arrived_sum(own_ref, ahead_ref, behind_ref, plus_ref, minus_ref):
    total = own_ref[0].astype(F32)
    for part in (ahead_ref[1], behind_ref[1], plus_ref[...], minus_ref[...]):
        total = total + part.astype(F32)
    return total


def activate_kernel(pre_ref, out_ref):
    gate, up = pre_ref[0].astype(F32), pre_ref[1].astype(F32)
    out_ref[...] = (gate / (1.0 + jnp.exp(-gate)) * up).astype(BF)


def grad_sum_kernel(*refs):
    refs[-1][...] = arrived_sum(*refs[:-1]).astype(BF)


def pack_kernel(core_ref, own_ref, low_ref, high_ref, ahead_ref, behind_ref, across_ref):
    ahead_ref[0] = own_ref[...]
    ahead_ref[1] = low_ref[...]
    behind_ref[0] = own_ref[...]
    behind_ref[1] = high_ref[...]
    across_ref[...] = jnp.where(core_ref[0] == 0, low_ref[...], high_ref[...])


def down_kernel(h_ref, w_ref, out_ref):
    blocks = h_ref.shape[0]
    h = jnp.concatenate([h_ref[i] for i in range(blocks)], axis=1)
    out_ref[...] = dot(h, w_ref[...], 1, 0).astype(BF)


def input_grad_kernel(
    place_ref, own_ref, low_ref, high_ref, ahead_ref, behind_ref, across_ref, slope_ref, w_ref, out_ref
):
    blocks = [ahead_ref.at[1], ahead_ref.at[0], behind_ref.at[1], behind_ref.at[0], across_ref, own_ref, high_ref, low_ref]
    source = [2, 3, 0, 1, 4, 5, 6, 7]
    unit = own_ref.shape[-1]
    total = None
    for block, i in zip(blocks, source):
        at = place_ref[i]
        columns = pl.ds(pl.multiple_of(at * unit, unit), unit)
        w = jnp.concatenate([w_ref[0, :, columns], w_ref[1, :, columns]], axis=1)
        h = block[...].astype(F32)
        d = jnp.concatenate([(h * slope_ref[at, g].astype(F32)).astype(BF) for g in range(2)], axis=1)
        part = dot(d, w, 1, 1)
        total = part if total is None else total + part
    out_ref[...] = total.astype(BF)


def rotated(value, steps, mirrored=False):
    nodes, count = lax.axis_size("node"), lax.axis_size("local")
    pairs = []
    for node in range(nodes):
        way = -steps if mirrored and node % 2 else steps
        pairs += [(node * count + i, node * count + (i + way) % count) for i in range(count)]
    return lax.ppermute(value, ("node", "local"), pairs)


def slope_kernel(saved_ref, out_ref):
    gate = saved_ref[0].astype(F32)
    up = saved_ref[1].astype(F32)
    sigma = 1.0 / (1.0 + jnp.exp(-gate))
    out_ref[0] = (up * sigma * (1.0 + gate * (1.0 - sigma))).T.astype(BF)
    out_ref[1] = (gate * sigma).T.astype(BF)


def shifted(value, axis, steps):
    count = lax.axis_size(axis)
    first, last = (max(0, -steps), min(count, count - steps))
    return lax.ppermute(value, axis, [(source, source + steps) for source in range(first, last)])


def rotated(value, steps, mirrored=False):
    nodes, count = lax.axis_size("node"), lax.axis_size("local")
    pairs = []
    for node in range(nodes):
        way = -steps if mirrored and node % 2 else steps
        pairs += [(node * count + i, node * count + (i + way) % count) for i in range(count)]
    return lax.ppermute(value, ("node", "local"), pairs)


def shifted(value, axis, steps):
    count = lax.axis_size(axis)
    first, last = (max(0, -steps), min(count, count - steps))
    return lax.ppermute(value, axis, [(source, source + steps) for source in range(first, last)])


def exchange(value, axis):
    return lax.all_to_all(value, axis, split_axis=0, concat_axis=0, tiled=True)


def body(inputs_b, grads_a, experts_a, experts_b, gates_a, gates_b, w_gate_up, w_down, saved_a):
    nodes, locals_ = lax.axis_size("node"), lax.axis_size("local")
    tokens, width = inputs_b.shape[1:]
    slots = saved_a.shape[4]
    cap = slots // nodes
    units = saved_a.shape[3]
    ids_a, ids_b = experts_a[0].T, experts_b[0].T
    gate_a, gate_b = gates_a[0].T, gates_b[0].T
    w_out = w_down[0, 0]
    w_in = w_gate_up[0, 0].transpose(1, 0, 2)

    def dispatch(ids, gates, x, gate_rows):
        return call(
            functools.partial(dispatch_kernel, nodes, cap, gate_rows),
            shape((slots, width)),
            (ids, gates, x),
            flops=2 * slots * tokens * width,
        )

    def combine_table(ids, gates, gate_rows):
        return call(
            functools.partial(combine_table_kernel, nodes, cap, gate_rows),
            shape((1 if gate_rows else 2, tokens, slots)),
            (ids, gates),
            flops=10**6,
        )

    def combine(table, rows):
        return call(combine_kernel, shape((tokens, width)), (table, rows), flops=2 * tokens * slots * width)

    me = lax.axis_index("local").astype(jnp.int32)
    core = (lax.axis_index("node") % 2).astype(jnp.int32).reshape(1)
    place = (me + jnp.array(LOCAL_ORDER, jnp.int32)) % locals_

    def partials(kernel, block, x, w):
        kinds = [shape(lead + block) for lead in ((2,), (2,), (), (3,))]
        flops = 2 * width * locals_ * functools.reduce(lambda a, b: a * b, block)
        return call(kernel, kinds, (place, x, w), flops=flops, scalars=True)

    def relay_sum(own, ahead, behind, across):
        kind = shape(across.shape)
        return call(relay_sum_kernel, (kind, kind), (core, own, ahead, behind, across), flops=10**6, scalars=True)

    def gather_local(own, other):
        low, high = rotated(own, 2), rotated(own, -2)
        two, one = shape((2,) + own.shape), shape(own.shape)
        ahead, behind, across = call(pack_kernel, (two, two, one), (core, own, low, high), scalars=True)
        ahead, behind, across, other = lax.optimization_barrier((ahead, behind, across, other))
        across = rotated(across, 2, True)
        return (own, low, high, rotated(ahead, 1), rotated(behind, -1), across), other

    send_a = dispatch(ids_a, gate_a, grads_a[0], True)
    rows_a = exchange(send_a, "node")
    send_b = dispatch(ids_b, gate_b, inputs_b[0], False)
    slope = call(slope_kernel, shape((2, slots, units)), (saved_a[0, 0],), flops=10**6)
    table_a = combine_table(ids_a, gate_a, True)
    table_b = combine_table(ids_b, gate_b, False)
    slopes = lax.all_gather(slope, "local", axis=0, tiled=True).reshape(locals_, 2, slots, units)
    send_b, w_in, table_a, table_b = lax.optimization_barrier((send_b, w_in, table_a, table_b))
    rows_b = exchange(send_b, "node")
    ahead, behind, across, own = partials(grad_hidden_kernel, (slots, units), rows_a, w_out)
    across = rotated(across, -2, True)
    ahead = rotated(ahead, 1)
    behind = rotated(behind, -1)
    half = 2
    part_b = call(
        up_kernel,
        shape((locals_, 2, slots, units)),
        (rows_b, w_in),
        flops=4 * slots * width * units * locals_,
        grid=(locals_ // half,),
        in_specs=[
            pl.BlockSpec((slots, width), lambda i: (0, 0)),
            pl.BlockSpec((2, width, half * units), lambda i: (0, 0, i)),
        ],
        out_specs=pl.BlockSpec((half, 2, slots, units), lambda i: (i, 0, 0, 0)),
    )
    ahead, behind, across, part_b, slopes = lax.optimization_barrier((ahead, behind, across, part_b, slopes))
    plus, minus = relay_sum(own, ahead, behind, across)
    pre_b = lax.psum_scatter(
        part_b.reshape(locals_, 2 * slots, units), "local", scatter_dimension=0, tiled=True
    ).reshape(2, slots, units)
    sums_a = (own, ahead, behind, rotated(plus, 2), rotated(minus, -2))
    grad_hidden = call(grad_sum_kernel, shape((slots, units)), sums_a, flops=10**6)
    grad_hidden, pre_b = gather_local(grad_hidden, pre_b)
    result_a = call(
        input_grad_kernel,
        shape((slots, width)),
        (place, *grad_hidden, slopes, w_in),
        flops=4 * slots * width * units * locals_,
        scalars=True,
    )
    hidden = call(activate_kernel, shape((slots, units)), (pre_b,), flops=10**6, limit=VMEM_WHOLE)
    hidden_all = lax.all_gather(hidden, "local", axis=0, tiled=True).reshape(locals_, slots, units)
    result_b = call(
        down_kernel,
        shape((slots, width)),
        (hidden_all, w_out),
        flops=2 * slots * width * units * locals_,
        limit=VMEM_WHOLE,
    )
    returned_a = exchange(result_a, "node")
    returned_a, result_b = lax.optimization_barrier((returned_a, result_b))
    returned_b = exchange(result_b, "node")
    input_grad = combine(table_a, returned_a)
    grads_prev = shifted(input_grad[None], "section", -1)
    outputs = combine(table_b, returned_b)
    return (outputs[None], grads_prev)


def solution(mesh):
    return jax.shard_map(
        body,
        mesh=mesh,
        in_specs=(
            P("section", "node", "local"),
            P("section", "node", "local"),
            P("section", "node", None),
            P("section", "node", None),
            P("section", "node", None),
            P("section", "node", None),
            P("section", "node", "local", None, None),
            P("section", "node", None, "local"),
            P("section", "node", None, "local", None),
        ),
        out_specs=(P("section", "node", "local"), P("section", "node", "local")),
        check_vma=False,
    )
```

```python
import functools

import jax
import jax.numpy as jnp
from jax import lax
from jax.experimental import pallas as pl
from jax.experimental.pallas import tpu as pltpu
from jax.sharding import PartitionSpec as P

BF = jnp.bfloat16
F32 = jnp.float32
VMEM_LIMIT = 48 * 1024 * 1024
VMEM_WHOLE = 60 * 1024 * 1024
LOCAL_ORDER = (3, 1, -3, -1, 4, 0, 2, -2)


def call(kernel, outs, args, flops=0, grid=None, in_specs=None, out_specs=None, scratch=(), scalars=False, limit=VMEM_LIMIT):
    moved = sum(a.size * a.dtype.itemsize for a in args)
    moved += sum(o.size * o.dtype.itemsize for o in jax.tree.leaves(outs))
    extra = {}
    if grid is not None:
        extra = dict(grid=grid, in_specs=in_specs, out_specs=out_specs)
    elif scalars:
        smem, vmem = pl.BlockSpec(memory_space=pltpu.SMEM), pl.BlockSpec(memory_space=pltpu.VMEM)
        extra = dict(in_specs=[smem] + [vmem] * (len(args) - 1))
    return pl.pallas_call(
        kernel,
        out_shape=outs,
        scratch_shapes=scratch,
        compiler_params=pltpu.CompilerParams(vmem_limit_bytes=limit),
        cost_estimate=pl.CostEstimate(flops=flops, bytes_accessed=moved, transcendentals=0),
        **extra,
    )(*args)


def shape(dims, dtype=BF):
    return jax.ShapeDtypeStruct(dims, dtype)


def dot(a, b, ca, cb):
    return lax.dot_general(a, b, (((ca,), (cb,)), ((), ())), preferred_element_type=F32)


def slot_table(ids_ref, gates_ref, experts, cap):
    top, tokens = ids_ref.shape
    expert = lax.broadcasted_iota(jnp.int32, (experts, tokens), 0)
    named = jnp.zeros((experts, tokens), F32)
    gate = jnp.zeros((experts, tokens), F32)
    for k in range(top):
        hit = (ids_ref[k : k + 1, :] == expert).astype(F32)
        named = named + hit
        gate = gate + hit * gates_ref[k : k + 1, :]
    earlier = lax.broadcasted_iota(jnp.int32, (tokens, tokens), 0) < lax.broadcasted_iota(
        jnp.int32, (tokens, tokens), 1
    )
    position = dot(named.astype(BF), earlier.astype(F32).astype(BF), 1, 0)
    position = jnp.where(named > 0, position, -1.0)
    slot = lax.broadcasted_iota(jnp.int32, (cap, tokens), 0).astype(F32)
    rows, gated = [], []
    for e in range(experts):
        fill = (position[e : e + 1, :] == slot).astype(F32)
        rows.append(fill)
        gated.append(fill * gate[e : e + 1, :])
    return jnp.concatenate(rows, axis=0), jnp.concatenate(gated, axis=0)


def dispatch_kernel(experts, cap, gate_rows, ids_ref, gates_ref, x_ref, out_ref):
    rows, gated = slot_table(ids_ref, gates_ref, experts, cap)
    picked = dot(rows.astype(BF), x_ref[...], 1, 0)
    if gate_rows:
        picked = picked * jnp.sum(gated, axis=1, keepdims=True)
    out_ref[...] = picked.astype(BF)


def combine_table_kernel(experts, cap, gate_rows, ids_ref, gates_ref, out_ref):
    rows, gated = slot_table(ids_ref, gates_ref, experts, cap)
    if gate_rows:
        out_ref[0] = rows.T.astype(BF)
    else:
        weight = gated.T
        high = weight.astype(BF)
        out_ref[0] = high
        out_ref[1] = (weight - high.astype(F32)).astype(BF)


def first_kernel(experts, cap, ids_ref, gates_ref, x_ref, saved_ref, out_ref, slope_ref):
    dispatch_kernel(experts, cap, True, ids_ref, gates_ref, x_ref, out_ref)
    slope_kernel(saved_ref, slope_ref)


def combine_kernel(table_ref, rows_ref, out_ref):
    total = dot(table_ref[0], rows_ref[...], 1, 0)
    for i in range(1, table_ref.shape[0]):
        total = total + dot(table_ref[i], rows_ref[...], 1, 0)
    out_ref[...] = total.astype(BF)


def spread_refs(ahead_ref, behind_ref, across_ref, own_ref):
    return [ahead_ref.at[0], ahead_ref.at[1], behind_ref.at[0], behind_ref.at[1], across_ref, *[own_ref.at[i] for i in range(3)]]


def up_kernel(x_ref, w_ref, out_ref):
    count = out_ref.shape[0]
    for j in range(count):
        w = jnp.concatenate([w_ref[0, :, 128 * j : 128 * j + 128], w_ref[1, :, 128 * j : 128 * j + 128]], axis=1)
        part = dot(x_ref[...], w, 1, 0).astype(BF)
        out_ref[j, 0] = part[:, :128]
        out_ref[j, 1] = part[:, 128:]


def grad_hidden_kernel(place_ref, x_ref, w_ref, *out_refs):
    outs = spread_refs(*out_refs)
    unit = outs[0].shape[-1]
    for i in range(0, len(outs), 2):
        w = jnp.concatenate(
            [w_ref[pl.ds(pl.multiple_of(place_ref[i + j] * unit, unit), unit), :] for j in range(2)], axis=0
        )
        part = dot(x_ref[...], w, 1, 1).astype(BF)
        outs[i][...] = part[:, :unit]
        outs[i + 1][...] = part[:, unit:]


def relay_sum_kernel(core_ref, own_ref, ahead_ref, behind_ref, across_ref, plus_ref, minus_ref):
    plus = own_ref[1].astype(F32) + ahead_ref[0].astype(F32)
    minus = own_ref[2].astype(F32) + behind_ref[0].astype(F32)
    across = across_ref[...].astype(F32)
    first = core_ref[0] == 0
    zero = jnp.zeros_like(across)
    plus_ref[...] = (plus + jnp.where(first, zero, across)).astype(BF)
    minus_ref[...] = (minus + jnp.where(first, across, zero)).astype(BF)


def arrived_sum(own_ref, ahead_ref, behind_ref, plus_ref, minus_ref):
    total = own_ref[0].astype(F32)
    for part in (ahead_ref[1], behind_ref[1], plus_ref[...], minus_ref[...]):
        total = total + part.astype(F32)
    return total


def activate_kernel(pre_ref, out_ref):
    gate, up = pre_ref[0].astype(F32), pre_ref[1].astype(F32)
    out_ref[...] = (gate / (1.0 + jnp.exp(-gate)) * up).astype(BF)


def grad_sum_kernel(*refs):
    refs[-1][...] = arrived_sum(*refs[:-1]).astype(BF)


def pack_kernel(core_ref, own_ref, low_ref, high_ref, ahead_ref, behind_ref, across_ref):
    ahead_ref[0] = own_ref[...]
    ahead_ref[1] = low_ref[...]
    behind_ref[0] = own_ref[...]
    behind_ref[1] = high_ref[...]
    across_ref[...] = jnp.where(core_ref[0] == 0, low_ref[...], high_ref[...])


def down_kernel(h_ref, w_ref, out_ref):
    blocks = h_ref.shape[0]
    h = jnp.concatenate([h_ref[i] for i in range(blocks)], axis=1)
    out_ref[...] = dot(h, w_ref[...], 1, 0).astype(BF)


def input_grad_kernel(
    place_ref, own_ref, low_ref, high_ref, ahead_ref, behind_ref, across_ref, slope_ref, w_ref, out_ref
):
    blocks = [ahead_ref.at[1], ahead_ref.at[0], behind_ref.at[1], behind_ref.at[0], across_ref, own_ref, high_ref, low_ref]
    source = [2, 3, 0, 1, 4, 5, 6, 7]
    unit = own_ref.shape[-1]
    total = None
    for block, i in zip(blocks, source):
        at = place_ref[i]
        columns = pl.ds(pl.multiple_of(at * unit, unit), unit)
        w = jnp.concatenate([w_ref[0, :, columns], w_ref[1, :, columns]], axis=1)
        h = block[...].astype(F32)
        d = jnp.concatenate([(h * slope_ref[at, g].astype(F32)).astype(BF) for g in range(2)], axis=1)
        part = dot(d, w, 1, 1)
        total = part if total is None else total + part
    out_ref[...] = total.astype(BF)


def rotated(value, steps, mirrored=False):
    nodes, count = lax.axis_size("node"), lax.axis_size("local")
    pairs = []
    for node in range(nodes):
        way = -steps if mirrored and node % 2 else steps
        pairs += [(node * count + i, node * count + (i + way) % count) for i in range(count)]
    return lax.ppermute(value, ("node", "local"), pairs)


def slope_kernel(saved_ref, out_ref):
    gate = saved_ref[0].astype(F32)
    up = saved_ref[1].astype(F32)
    sigma = 1.0 / (1.0 + jnp.exp(-gate))
    out_ref[0] = (up * sigma * (1.0 + gate * (1.0 - sigma))).T.astype(BF)
    out_ref[1] = (gate * sigma).T.astype(BF)


def shifted(value, axis, steps):
    count = lax.axis_size(axis)
    first, last = (max(0, -steps), min(count, count - steps))
    return lax.ppermute(value, axis, [(source, source + steps) for source in range(first, last)])


def rotated(value, steps, mirrored=False):
    nodes, count = lax.axis_size("node"), lax.axis_size("local")
    pairs = []
    for node in range(nodes):
        way = -steps if mirrored and node % 2 else steps
        pairs += [(node * count + i, node * count + (i + way) % count) for i in range(count)]
    return lax.ppermute(value, ("node", "local"), pairs)


def shifted(value, axis, steps):
    count = lax.axis_size(axis)
    first, last = (max(0, -steps), min(count, count - steps))
    return lax.ppermute(value, axis, [(source, source + steps) for source in range(first, last)])


def exchange(value, axis):
    return lax.all_to_all(value, axis, split_axis=0, concat_axis=0, tiled=True)


def body(inputs_b, grads_a, experts_a, experts_b, gates_a, gates_b, w_gate_up, w_down, saved_a):
    nodes, locals_ = lax.axis_size("node"), lax.axis_size("local")
    tokens, width = inputs_b.shape[1:]
    slots = saved_a.shape[4]
    cap = slots // nodes
    units = saved_a.shape[3]
    ids_a, ids_b = experts_a[0].T, experts_b[0].T
    gate_a, gate_b = gates_a[0].T, gates_b[0].T
    w_out = w_down[0, 0]
    w_in = w_gate_up[0, 0].transpose(1, 0, 2)

    def dispatch(ids, gates, x, gate_rows):
        return call(
            functools.partial(dispatch_kernel, nodes, cap, gate_rows),
            shape((slots, width)),
            (ids, gates, x),
            flops=2 * slots * tokens * width,
        )

    def combine_table(ids, gates, gate_rows):
        return call(
            functools.partial(combine_table_kernel, nodes, cap, gate_rows),
            shape((1 if gate_rows else 2, tokens, slots)),
            (ids, gates),
            flops=10**6,
        )

    def combine(table, rows):
        return call(combine_kernel, shape((tokens, width)), (table, rows), flops=2 * tokens * slots * width)

    me = lax.axis_index("local").astype(jnp.int32)
    core = (lax.axis_index("node") % 2).astype(jnp.int32).reshape(1)
    place = (me + jnp.array(LOCAL_ORDER, jnp.int32)) % locals_

    def partials(kernel, block, x, w):
        kinds = [shape(lead + block) for lead in ((2,), (2,), (), (3,))]
        flops = 2 * width * locals_ * functools.reduce(lambda a, b: a * b, block)
        return call(kernel, kinds, (place, x, w), flops=flops, scalars=True)

    def relay_sum(own, ahead, behind, across):
        kind = shape(across.shape)
        return call(relay_sum_kernel, (kind, kind), (core, own, ahead, behind, across), flops=10**6, scalars=True)

    def gather_local(own, other):
        low, high = rotated(own, 2), rotated(own, -2)
        two, one = shape((2,) + own.shape), shape(own.shape)
        ahead, behind, across = call(pack_kernel, (two, two, one), (core, own, low, high), scalars=True)
        ahead, behind, across, other = lax.optimization_barrier((ahead, behind, across, other))
        across = rotated(across, 2, True)
        return (own, low, high, rotated(ahead, 1), rotated(behind, -1), across), other

    send_a, slope = call(
        functools.partial(first_kernel, nodes, cap),
        (shape((slots, width)), shape((2, slots, units))),
        (ids_a, gate_a, grads_a[0], saved_a[0, 0]),
        flops=2 * slots * tokens * width,
        limit=VMEM_WHOLE,
    )
    rows_a = exchange(send_a, "node")
    send_b = dispatch(ids_b, gate_b, inputs_b[0], False)
    table_a = combine_table(ids_a, gate_a, True)
    table_b = combine_table(ids_b, gate_b, False)
    slopes = lax.all_gather(slope, "local", axis=0, tiled=True).reshape(locals_, 2, slots, units)
    send_b, w_in, table_a, table_b = lax.optimization_barrier((send_b, w_in, table_a, table_b))
    rows_b = exchange(send_b, "node")
    ahead, behind, across, own = partials(grad_hidden_kernel, (slots, units), rows_a, w_out)
    across = rotated(across, -2, True)
    ahead = rotated(ahead, 1)
    behind = rotated(behind, -1)
    half = 2
    part_b = call(
        up_kernel,
        shape((locals_, 2, slots, units)),
        (rows_b, w_in),
        flops=4 * slots * width * units * locals_,
        grid=(locals_ // half,),
        in_specs=[
            pl.BlockSpec((slots, width), lambda i: (0, 0)),
            pl.BlockSpec((2, width, half * units), lambda i: (0, 0, i)),
        ],
        out_specs=pl.BlockSpec((half, 2, slots, units), lambda i: (i, 0, 0, 0)),
    )
    ahead, behind, across, part_b, slopes = lax.optimization_barrier((ahead, behind, across, part_b, slopes))
    plus, minus = relay_sum(own, ahead, behind, across)
    pre_b = lax.psum_scatter(
        part_b.reshape(locals_, 2 * slots, units), "local", scatter_dimension=0, tiled=True
    ).reshape(2, slots, units)
    sums_a = (own, ahead, behind, rotated(plus, 2), rotated(minus, -2))
    grad_hidden = call(grad_sum_kernel, shape((slots, units)), sums_a, flops=10**6)
    grad_hidden, pre_b = gather_local(grad_hidden, pre_b)
    result_a = call(
        input_grad_kernel,
        shape((slots, width)),
        (place, *grad_hidden, slopes, w_in),
        flops=4 * slots * width * units * locals_,
        scalars=True,
    )
    hidden = call(activate_kernel, shape((slots, units)), (pre_b,), flops=10**6, limit=VMEM_WHOLE)
    hidden_all = lax.all_gather(hidden, "local", axis=0, tiled=True).reshape(locals_, slots, units)
    result_b = call(
        down_kernel,
        shape((slots, width)),
        (hidden_all, w_out),
        flops=2 * slots * width * units * locals_,
        limit=VMEM_WHOLE,
    )
    returned_a = exchange(result_a, "node")
    returned_a, result_b = lax.optimization_barrier((returned_a, result_b))
    returned_b = exchange(result_b, "node")
    input_grad = combine(table_a, returned_a)
    grads_prev = shifted(input_grad[None], "section", -1)
    outputs = combine(table_b, returned_b)
    return (outputs[None], grads_prev)


def solution(mesh):
    return jax.shard_map(
        body,
        mesh=mesh,
        in_specs=(
            P("section", "node", "local"),
            P("section", "node", "local"),
            P("section", "node", None),
            P("section", "node", None),
            P("section", "node", None),
            P("section", "node", None),
            P("section", "node", "local", None, None),
            P("section", "node", None, "local"),
            P("section", "node", None, "local", None),
        ),
        out_specs=(P("section", "node", "local"), P("section", "node", "local")),
        check_vma=False,
    )
```

```python
import functools

import jax
import jax.numpy as jnp
from jax import lax
from jax.experimental import pallas as pl
from jax.experimental.pallas import tpu as pltpu
from jax.sharding import PartitionSpec as P

BF = jnp.bfloat16
F32 = jnp.float32
VMEM_LIMIT = 48 * 1024 * 1024
VMEM_WHOLE = 60 * 1024 * 1024
LOCAL_ORDER = (3, 1, -3, -1, 4, 0, 2, -2)


def call(kernel, outs, args, flops=0, grid=None, in_specs=None, out_specs=None, scratch=(), scalars=False, limit=VMEM_LIMIT):
    moved = sum(a.size * a.dtype.itemsize for a in args)
    moved += sum(o.size * o.dtype.itemsize for o in jax.tree.leaves(outs))
    extra = {}
    if grid is not None:
        extra = dict(grid=grid, in_specs=in_specs, out_specs=out_specs)
    elif scalars:
        smem, vmem = pl.BlockSpec(memory_space=pltpu.SMEM), pl.BlockSpec(memory_space=pltpu.VMEM)
        extra = dict(in_specs=[smem] + [vmem] * (len(args) - 1))
    return pl.pallas_call(
        kernel,
        out_shape=outs,
        scratch_shapes=scratch,
        compiler_params=pltpu.CompilerParams(vmem_limit_bytes=limit),
        cost_estimate=pl.CostEstimate(flops=flops, bytes_accessed=moved, transcendentals=0),
        **extra,
    )(*args)


def shape(dims, dtype=BF):
    return jax.ShapeDtypeStruct(dims, dtype)


def dot(a, b, ca, cb):
    return lax.dot_general(a, b, (((ca,), (cb,)), ((), ())), preferred_element_type=F32)


def slot_table(ids_ref, gates_ref, experts, cap):
    top, tokens = ids_ref.shape
    expert = lax.broadcasted_iota(jnp.int32, (experts, tokens), 0)
    named = jnp.zeros((experts, tokens), F32)
    gate = jnp.zeros((experts, tokens), F32)
    for k in range(top):
        hit = (ids_ref[k : k + 1, :] == expert).astype(F32)
        named = named + hit
        gate = gate + hit * gates_ref[k : k + 1, :]
    earlier = lax.broadcasted_iota(jnp.int32, (tokens, tokens), 0) < lax.broadcasted_iota(
        jnp.int32, (tokens, tokens), 1
    )
    position = dot(named.astype(BF), earlier.astype(F32).astype(BF), 1, 0)
    position = jnp.where(named > 0, position, -1.0)
    slot = lax.broadcasted_iota(jnp.int32, (cap, tokens), 0).astype(F32)
    rows, gated = [], []
    for e in range(experts):
        fill = (position[e : e + 1, :] == slot).astype(F32)
        rows.append(fill)
        gated.append(fill * gate[e : e + 1, :])
    return jnp.concatenate(rows, axis=0), jnp.concatenate(gated, axis=0)


def dispatch_kernel(experts, cap, gate_rows, ids_ref, gates_ref, x_ref, out_ref):
    rows, gated = slot_table(ids_ref, gates_ref, experts, cap)
    picked = dot(rows.astype(BF), x_ref[...], 1, 0)
    if gate_rows:
        picked = picked * jnp.sum(gated, axis=1, keepdims=True)
    out_ref[...] = picked.astype(BF)


def combine_table_kernel(experts, cap, gate_rows, ids_ref, gates_ref, out_ref):
    rows, gated = slot_table(ids_ref, gates_ref, experts, cap)
    if gate_rows:
        out_ref[0] = rows.T.astype(BF)
    else:
        weight = gated.T
        high = weight.astype(BF)
        out_ref[0] = high
        out_ref[1] = (weight - high.astype(F32)).astype(BF)


def first_kernel(experts, cap, ids_ref, gates_ref, x_ref, saved_ref, out_ref, slope_ref):
    dispatch_kernel(experts, cap, True, ids_ref, gates_ref, x_ref, out_ref)
    slope_kernel(saved_ref, slope_ref)


def combine_kernel(table_ref, rows_ref, out_ref):
    total = dot(table_ref[0], rows_ref[...], 1, 0)
    for i in range(1, table_ref.shape[0]):
        total = total + dot(table_ref[i], rows_ref[...], 1, 0)
    out_ref[...] = total.astype(BF)


def spread_refs(ahead_ref, behind_ref, across_ref, own_ref):
    return [ahead_ref.at[0], ahead_ref.at[1], behind_ref.at[0], behind_ref.at[1], across_ref, *[own_ref.at[i] for i in range(3)]]


def up_kernel(x_ref, w_ref, out_ref):
    count = out_ref.shape[0]
    for j in range(count):
        w = jnp.concatenate([w_ref[0, :, 128 * j : 128 * j + 128], w_ref[1, :, 128 * j : 128 * j + 128]], axis=1)
        part = dot(x_ref[...], w, 1, 0).astype(BF)
        out_ref[j, 0] = part[:, :128]
        out_ref[j, 1] = part[:, 128:]


def grad_hidden_kernel(place_ref, x_ref, w_ref, *out_refs):
    outs = spread_refs(*out_refs)
    unit = outs[0].shape[-1]
    for i in range(0, len(outs), 2):
        w = jnp.concatenate(
            [w_ref[pl.ds(pl.multiple_of(place_ref[i + j] * unit, unit), unit), :] for j in range(2)], axis=0
        )
        part = dot(x_ref[...], w, 1, 1).astype(BF)
        outs[i][...] = part[:, :unit]
        outs[i + 1][...] = part[:, unit:]


def relay_sum_kernel(core_ref, own_ref, ahead_ref, behind_ref, across_ref, plus_ref, minus_ref):
    plus = own_ref[1].astype(F32) + ahead_ref[0].astype(F32)
    minus = own_ref[2].astype(F32) + behind_ref[0].astype(F32)
    across = across_ref[...].astype(F32)
    first = core_ref[0] == 0
    zero = jnp.zeros_like(across)
    plus_ref[...] = (plus + jnp.where(first, zero, across)).astype(BF)
    minus_ref[...] = (minus + jnp.where(first, across, zero)).astype(BF)


def arrived_sum(own_ref, ahead_ref, behind_ref, plus_ref, minus_ref):
    total = own_ref[0].astype(F32)
    for part in (ahead_ref[1], behind_ref[1], plus_ref[...], minus_ref[...]):
        total = total + part.astype(F32)
    return total


def activate_kernel(pre_ref, out_ref):
    gate, up = pre_ref[0].astype(F32), pre_ref[1].astype(F32)
    out_ref[...] = (gate / (1.0 + jnp.exp(-gate)) * up).astype(BF)


def grad_sum_kernel(*refs):
    refs[-1][...] = arrived_sum(*refs[:-1]).astype(BF)


def pack_kernel(core_ref, own_ref, low_ref, high_ref, ahead_ref, behind_ref, across_ref):
    ahead_ref[0] = own_ref[...]
    ahead_ref[1] = low_ref[...]
    behind_ref[0] = own_ref[...]
    behind_ref[1] = high_ref[...]
    across_ref[...] = jnp.where(core_ref[0] == 0, low_ref[...], high_ref[...])


def down_kernel(h_ref, w_ref, out_ref):
    blocks = h_ref.shape[0]
    h = jnp.concatenate([h_ref[i] for i in range(blocks)], axis=1)
    out_ref[...] = dot(h, w_ref[...], 1, 0).astype(BF)


def input_grad_kernel(
    place_ref, own_ref, low_ref, high_ref, ahead_ref, behind_ref, across_ref, slope_ref, w_ref, out_ref
):
    blocks = [ahead_ref.at[1], ahead_ref.at[0], behind_ref.at[1], behind_ref.at[0], across_ref, own_ref, high_ref, low_ref]
    source = [2, 3, 0, 1, 4, 5, 6, 7]
    unit = own_ref.shape[-1]
    total = None
    for block, i in zip(blocks, source):
        at = place_ref[i]
        columns = pl.ds(pl.multiple_of(at * unit, unit), unit)
        w = jnp.concatenate([w_ref[0, :, columns], w_ref[1, :, columns]], axis=1)
        h = block[...].astype(F32)
        d = jnp.concatenate([(h * slope_ref[at, g].astype(F32)).astype(BF) for g in range(2)], axis=1)
        part = dot(d, w, 1, 1)
        total = part if total is None else total + part
    out_ref[...] = total.astype(BF)


def rotated(value, steps, mirrored=False):
    nodes, count = lax.axis_size("node"), lax.axis_size("local")
    pairs = []
    for node in range(nodes):
        way = -steps if mirrored and node % 2 else steps
        pairs += [(node * count + i, node * count + (i + way) % count) for i in range(count)]
    return lax.ppermute(value, ("node", "local"), pairs)


def slope_kernel(saved_ref, out_ref):
    gate = saved_ref[0].astype(F32)
    up = saved_ref[1].astype(F32)
    sigma = 1.0 / (1.0 + jnp.exp(-gate))
    out_ref[0] = (up * sigma * (1.0 + gate * (1.0 - sigma))).T.astype(BF)
    out_ref[1] = (gate * sigma).T.astype(BF)


def shifted(value, axis, steps):
    count = lax.axis_size(axis)
    first, last = (max(0, -steps), min(count, count - steps))
    return lax.ppermute(value, axis, [(source, source + steps) for source in range(first, last)])


def rotated(value, steps, mirrored=False):
    nodes, count = lax.axis_size("node"), lax.axis_size("local")
    pairs = []
    for node in range(nodes):
        way = -steps if mirrored and node % 2 else steps
        pairs += [(node * count + i, node * count + (i + way) % count) for i in range(count)]
    return lax.ppermute(value, ("node", "local"), pairs)


def shifted(value, axis, steps):
    count = lax.axis_size(axis)
    first, last = (max(0, -steps), min(count, count - steps))
    return lax.ppermute(value, axis, [(source, source + steps) for source in range(first, last)])


def exchange(value, axis):
    return lax.all_to_all(value, axis, split_axis=0, concat_axis=0, tiled=True)


def body(inputs_b, grads_a, experts_a, experts_b, gates_a, gates_b, w_gate_up, w_down, saved_a):
    nodes, locals_ = lax.axis_size("node"), lax.axis_size("local")
    tokens, width = inputs_b.shape[1:]
    slots = saved_a.shape[4]
    cap = slots // nodes
    units = saved_a.shape[3]
    ids_a, ids_b = experts_a[0].T, experts_b[0].T
    gate_a, gate_b = gates_a[0].T, gates_b[0].T
    w_out = w_down[0, 0]
    w_in = w_gate_up[0, 0].transpose(1, 0, 2)

    def dispatch(ids, gates, x, gate_rows):
        return call(
            functools.partial(dispatch_kernel, nodes, cap, gate_rows),
            shape((slots, width)),
            (ids, gates, x),
            flops=2 * slots * tokens * width,
        )

    def combine_table(ids, gates, gate_rows):
        return call(
            functools.partial(combine_table_kernel, nodes, cap, gate_rows),
            shape((1 if gate_rows else 2, tokens, slots)),
            (ids, gates),
            flops=10**6,
        )

    def combine(table, rows):
        return call(combine_kernel, shape((tokens, width)), (table, rows), flops=2 * tokens * slots * width)

    me = lax.axis_index("local").astype(jnp.int32)
    core = (lax.axis_index("node") % 2).astype(jnp.int32).reshape(1)
    place = (me + jnp.array(LOCAL_ORDER, jnp.int32)) % locals_

    def partials(kernel, block, x, w):
        kinds = [shape(lead + block) for lead in ((2,), (2,), (), (3,))]
        flops = 2 * width * locals_ * functools.reduce(lambda a, b: a * b, block)
        return call(kernel, kinds, (place, x, w), flops=flops, scalars=True)

    def relay_sum(own, ahead, behind, across):
        kind = shape(across.shape)
        return call(relay_sum_kernel, (kind, kind), (core, own, ahead, behind, across), flops=10**6, scalars=True)

    def gather_local(own, other):
        low, high = rotated(own, 2), rotated(own, -2)
        two, one = shape((2,) + own.shape), shape(own.shape)
        ahead, behind, across = call(pack_kernel, (two, two, one), (core, own, low, high), scalars=True)
        across = rotated(across, 2, True)
        ahead, behind, across, other = lax.optimization_barrier((ahead, behind, across, other))
        return (own, low, high, rotated(ahead, 1), rotated(behind, -1), across), other

    send_a, slope = call(
        functools.partial(first_kernel, nodes, cap),
        (shape((slots, width)), shape((2, slots, units))),
        (ids_a, gate_a, grads_a[0], saved_a[0, 0]),
        flops=2 * slots * tokens * width,
        limit=VMEM_WHOLE,
    )
    rows_a = exchange(send_a, "node")
    send_b = dispatch(ids_b, gate_b, inputs_b[0], False)
    table_a = combine_table(ids_a, gate_a, True)
    table_b = combine_table(ids_b, gate_b, False)
    slopes = lax.all_gather(slope, "local", axis=0, tiled=True).reshape(locals_, 2, slots, units)
    send_b, w_in, table_a, table_b = lax.optimization_barrier((send_b, w_in, table_a, table_b))
    rows_b = exchange(send_b, "node")
    ahead, behind, across, own = partials(grad_hidden_kernel, (slots, units), rows_a, w_out)
    across = rotated(across, -2, True)
    ahead = rotated(ahead, 1)
    behind = rotated(behind, -1)
    half = 2
    part_b = call(
        up_kernel,
        shape((locals_, 2, slots, units)),
        (rows_b, w_in),
        flops=4 * slots * width * units * locals_,
        grid=(locals_ // half,),
        in_specs=[
            pl.BlockSpec((slots, width), lambda i: (0, 0)),
            pl.BlockSpec((2, width, half * units), lambda i: (0, 0, i)),
        ],
        out_specs=pl.BlockSpec((half, 2, slots, units), lambda i: (i, 0, 0, 0)),
    )
    ahead, behind, across, part_b, slopes = lax.optimization_barrier((ahead, behind, across, part_b, slopes))
    plus, minus = relay_sum(own, ahead, behind, across)
    pre_b = lax.psum_scatter(
        part_b.reshape(locals_, 2 * slots, units), "local", scatter_dimension=0, tiled=True
    ).reshape(2, slots, units)
    sums_a = (own, ahead, behind, rotated(plus, 2), rotated(minus, -2))
    grad_hidden = call(grad_sum_kernel, shape((slots, units)), sums_a, flops=10**6)
    grad_hidden, pre_b = gather_local(grad_hidden, pre_b)
    result_a = call(
        input_grad_kernel,
        shape((slots, width)),
        (place, *grad_hidden, slopes, w_in),
        flops=4 * slots * width * units * locals_,
        scalars=True,
    )
    hidden = call(activate_kernel, shape((slots, units)), (pre_b,), flops=10**6, limit=VMEM_WHOLE)
    hidden_all = lax.all_gather(hidden, "local", axis=0, tiled=True).reshape(locals_, slots, units)
    result_b = call(
        down_kernel,
        shape((slots, width)),
        (hidden_all, w_out),
        flops=2 * slots * width * units * locals_,
        limit=VMEM_WHOLE,
    )
    returned_a = exchange(result_a, "node")
    returned_a, result_b = lax.optimization_barrier((returned_a, result_b))
    returned_b = exchange(result_b, "node")
    input_grad = combine(table_a, returned_a)
    grads_prev = shifted(input_grad[None], "section", -1)
    outputs = combine(table_b, returned_b)
    return (outputs[None], grads_prev)


def solution(mesh):
    return jax.shard_map(
        body,
        mesh=mesh,
        in_specs=(
            P("section", "node", "local"),
            P("section", "node", "local"),
            P("section", "node", None),
            P("section", "node", None),
            P("section", "node", None),
            P("section", "node", None),
            P("section", "node", "local", None, None),
            P("section", "node", None, "local"),
            P("section", "node", None, "local", None),
        ),
        out_specs=(P("section", "node", "local"), P("section", "node", "local")),
        check_vma=False,
    )
```

```python
import functools

import jax
import jax.numpy as jnp
from jax import lax
from jax.experimental import pallas as pl
from jax.experimental.pallas import tpu as pltpu
from jax.sharding import PartitionSpec as P

BF = jnp.bfloat16
F32 = jnp.float32
VMEM_LIMIT = 48 * 1024 * 1024
VMEM_WHOLE = 60 * 1024 * 1024
LOCAL_ORDER = (3, 1, -3, -1, 4, 0, 2, -2)


def call(kernel, outs, args, flops=0, grid=None, in_specs=None, out_specs=None, scratch=(), scalars=False, limit=VMEM_LIMIT):
    moved = sum(a.size * a.dtype.itemsize for a in args)
    moved += sum(o.size * o.dtype.itemsize for o in jax.tree.leaves(outs))
    extra = {}
    if grid is not None:
        extra = dict(grid=grid, in_specs=in_specs, out_specs=out_specs)
    elif scalars:
        smem, vmem = pl.BlockSpec(memory_space=pltpu.SMEM), pl.BlockSpec(memory_space=pltpu.VMEM)
        extra = dict(in_specs=[smem] + [vmem] * (len(args) - 1))
    return pl.pallas_call(
        kernel,
        out_shape=outs,
        scratch_shapes=scratch,
        compiler_params=pltpu.CompilerParams(vmem_limit_bytes=limit),
        cost_estimate=pl.CostEstimate(flops=flops, bytes_accessed=moved, transcendentals=0),
        **extra,
    )(*args)


def shape(dims, dtype=BF):
    return jax.ShapeDtypeStruct(dims, dtype)


def dot(a, b, ca, cb):
    return lax.dot_general(a, b, (((ca,), (cb,)), ((), ())), preferred_element_type=F32)


def slot_table(ids_ref, gates_ref, experts, cap):
    top, tokens = ids_ref.shape
    expert = lax.broadcasted_iota(jnp.int32, (experts, tokens), 0)
    named = jnp.zeros((experts, tokens), F32)
    gate = jnp.zeros((experts, tokens), F32)
    for k in range(top):
        hit = (ids_ref[k : k + 1, :] == expert).astype(F32)
        named = named + hit
        gate = gate + hit * gates_ref[k : k + 1, :]
    earlier = lax.broadcasted_iota(jnp.int32, (tokens, tokens), 0) < lax.broadcasted_iota(
        jnp.int32, (tokens, tokens), 1
    )
    position = dot(named.astype(BF), earlier.astype(F32).astype(BF), 1, 0)
    position = jnp.where(named > 0, position, -1.0)
    slot = lax.broadcasted_iota(jnp.int32, (cap, tokens), 0).astype(F32)
    rows, gated = [], []
    for e in range(experts):
        fill = (position[e : e + 1, :] == slot).astype(F32)
        rows.append(fill)
        gated.append(fill * gate[e : e + 1, :])
    return jnp.concatenate(rows, axis=0), jnp.concatenate(gated, axis=0)


def dispatch_kernel(experts, cap, gate_rows, ids_ref, gates_ref, x_ref, out_ref):
    rows, gated = slot_table(ids_ref, gates_ref, experts, cap)
    picked = dot(rows.astype(BF), x_ref[...], 1, 0)
    if gate_rows:
        picked = picked * jnp.sum(gated, axis=1, keepdims=True)
    out_ref[...] = picked.astype(BF)


def combine_table_kernel(experts, cap, gate_rows, ids_ref, gates_ref, out_ref):
    rows, gated = slot_table(ids_ref, gates_ref, experts, cap)
    if gate_rows:
        out_ref[0] = rows.T.astype(BF)
    else:
        weight = gated.T
        high = weight.astype(BF)
        out_ref[0] = high
        out_ref[1] = (weight - high.astype(F32)).astype(BF)


def first_kernel(experts, cap, ids_ref, gates_ref, x_ref, saved_ref, out_ref, slope_ref):
    dispatch_kernel(experts, cap, True, ids_ref, gates_ref, x_ref, out_ref)
    slope_kernel(saved_ref, slope_ref)


def combine_kernel(table_ref, rows_ref, out_ref):
    total = dot(table_ref[0], rows_ref[...], 1, 0)
    for i in range(1, table_ref.shape[0]):
        total = total + dot(table_ref[i], rows_ref[...], 1, 0)
    out_ref[...] = total.astype(BF)


def spread_refs(ahead_ref, behind_ref, across_ref, own_ref):
    return [ahead_ref.at[0], ahead_ref.at[1], behind_ref.at[0], behind_ref.at[1], across_ref, *[own_ref.at[i] for i in range(3)]]


def up_kernel(x_ref, w_ref, out_ref):
    count = out_ref.shape[0]
    for j in range(count):
        w = jnp.concatenate([w_ref[0, :, 128 * j : 128 * j + 128], w_ref[1, :, 128 * j : 128 * j + 128]], axis=1)
        part = dot(x_ref[...], w, 1, 0).astype(BF)
        out_ref[j, 0] = part[:, :128]
        out_ref[j, 1] = part[:, 128:]


def grad_hidden_kernel(place_ref, x_ref, w_ref, *out_refs):
    outs = spread_refs(*out_refs)
    unit = outs[0].shape[-1]
    for i in range(0, len(outs), 2):
        w = jnp.concatenate(
            [w_ref[pl.ds(pl.multiple_of(place_ref[i + j] * unit, unit), unit), :] for j in range(2)], axis=0
        )
        part = dot(x_ref[...], w, 1, 1).astype(BF)
        outs[i][...] = part[:, :unit]
        outs[i + 1][...] = part[:, unit:]


def relay_sum_kernel(core_ref, own_ref, ahead_ref, behind_ref, across_ref, plus_ref, minus_ref):
    plus = own_ref[1].astype(F32) + ahead_ref[0].astype(F32)
    minus = own_ref[2].astype(F32) + behind_ref[0].astype(F32)
    across = across_ref[...].astype(F32)
    first = core_ref[0] == 0
    zero = jnp.zeros_like(across)
    plus_ref[...] = (plus + jnp.where(first, zero, across)).astype(BF)
    minus_ref[...] = (minus + jnp.where(first, across, zero)).astype(BF)


def arrived_sum(own_ref, ahead_ref, behind_ref, plus_ref, minus_ref):
    total = own_ref[0].astype(F32)
    for part in (ahead_ref[1], behind_ref[1], plus_ref[...], minus_ref[...]):
        total = total + part.astype(F32)
    return total


def activate_kernel(pre_ref, out_ref):
    gate, up = pre_ref[0].astype(F32), pre_ref[1].astype(F32)
    out_ref[...] = (gate / (1.0 + jnp.exp(-gate)) * up).astype(BF)


def grad_sum_kernel(*refs):
    refs[-1][...] = arrived_sum(*refs[:-1]).astype(BF)


def pack_kernel(core_ref, own_ref, low_ref, high_ref, ahead_ref, behind_ref, across_ref):
    ahead_ref[0] = own_ref[...]
    ahead_ref[1] = low_ref[...]
    behind_ref[0] = own_ref[...]
    behind_ref[1] = high_ref[...]
    across_ref[...] = jnp.where(core_ref[0] == 0, low_ref[...], high_ref[...])


def down_kernel(h_ref, w_ref, out_ref):
    blocks = h_ref.shape[0]
    h = jnp.concatenate([h_ref[i] for i in range(blocks)], axis=1)
    out_ref[...] = dot(h, w_ref[...], 1, 0).astype(BF)


def input_grad_kernel(
    place_ref, own_ref, low_ref, high_ref, ahead_ref, behind_ref, across_ref, slope_ref, w_ref, out_ref
):
    blocks = [ahead_ref.at[1], ahead_ref.at[0], behind_ref.at[1], behind_ref.at[0], across_ref, own_ref, high_ref, low_ref]
    source = [2, 3, 0, 1, 4, 5, 6, 7]
    unit = own_ref.shape[-1]
    total = None
    for block, i in zip(blocks, source):
        at = place_ref[i]
        columns = pl.ds(pl.multiple_of(at * unit, unit), unit)
        w = jnp.concatenate([w_ref[0, :, columns], w_ref[1, :, columns]], axis=1)
        h = block[...].astype(F32)
        d = jnp.concatenate([(h * slope_ref[at, g].astype(F32)).astype(BF) for g in range(2)], axis=1)
        part = dot(d, w, 1, 1)
        total = part if total is None else total + part
    out_ref[...] = total.astype(BF)


def rotated(value, steps, mirrored=False):
    nodes, count = lax.axis_size("node"), lax.axis_size("local")
    pairs = []
    for node in range(nodes):
        way = -steps if mirrored and node % 2 else steps
        pairs += [(node * count + i, node * count + (i + way) % count) for i in range(count)]
    return lax.ppermute(value, ("node", "local"), pairs)


def slope_kernel(saved_ref, out_ref):
    gate = saved_ref[0].astype(F32)
    up = saved_ref[1].astype(F32)
    sigma = 1.0 / (1.0 + jnp.exp(-gate))
    out_ref[0] = (up * sigma * (1.0 + gate * (1.0 - sigma))).T.astype(BF)
    out_ref[1] = (gate * sigma).T.astype(BF)


def shifted(value, axis, steps):
    count = lax.axis_size(axis)
    first, last = (max(0, -steps), min(count, count - steps))
    return lax.ppermute(value, axis, [(source, source + steps) for source in range(first, last)])


def rotated(value, steps, mirrored=False):
    nodes, count = lax.axis_size("node"), lax.axis_size("local")
    pairs = []
    for node in range(nodes):
        way = -steps if mirrored and node % 2 else steps
        pairs += [(node * count + i, node * count + (i + way) % count) for i in range(count)]
    return lax.ppermute(value, ("node", "local"), pairs)


def shifted(value, axis, steps):
    count = lax.axis_size(axis)
    first, last = (max(0, -steps), min(count, count - steps))
    return lax.ppermute(value, axis, [(source, source + steps) for source in range(first, last)])


def exchange(value, axis):
    return lax.all_to_all(value, axis, split_axis=0, concat_axis=0, tiled=True)


def body(inputs_b, grads_a, experts_a, experts_b, gates_a, gates_b, w_gate_up, w_down, saved_a):
    nodes, locals_ = lax.axis_size("node"), lax.axis_size("local")
    tokens, width = inputs_b.shape[1:]
    slots = saved_a.shape[4]
    cap = slots // nodes
    units = saved_a.shape[3]
    ids_a, ids_b = experts_a[0].T, experts_b[0].T
    gate_a, gate_b = gates_a[0].T, gates_b[0].T
    w_out = w_down[0, 0]
    w_in = w_gate_up[0, 0].transpose(1, 0, 2)

    def dispatch(ids, gates, x, gate_rows):
        return call(
            functools.partial(dispatch_kernel, nodes, cap, gate_rows),
            shape((slots, width)),
            (ids, gates, x),
            flops=2 * slots * tokens * width,
        )

    def combine_table(ids, gates, gate_rows):
        return call(
            functools.partial(combine_table_kernel, nodes, cap, gate_rows),
            shape((1 if gate_rows else 2, tokens, slots)),
            (ids, gates),
            flops=10**6,
        )

    def combine(table, rows):
        return call(combine_kernel, shape((tokens, width)), (table, rows), flops=2 * tokens * slots * width)

    me = lax.axis_index("local").astype(jnp.int32)
    core = (lax.axis_index("node") % 2).astype(jnp.int32).reshape(1)
    place = (me + jnp.array(LOCAL_ORDER, jnp.int32)) % locals_

    def partials(kernel, block, x, w):
        kinds = [shape(lead + block) for lead in ((2,), (2,), (), (3,))]
        flops = 2 * width * locals_ * functools.reduce(lambda a, b: a * b, block)
        return call(kernel, kinds, (place, x, w), flops=flops, scalars=True, limit=VMEM_WHOLE)

    def relay_sum(own, ahead, behind, across):
        kind = shape(across.shape)
        return call(relay_sum_kernel, (kind, kind), (core, own, ahead, behind, across), flops=10**6, scalars=True)

    def gather_local(own, other):
        low, high = rotated(own, 2), rotated(own, -2)
        two, one = shape((2,) + own.shape), shape(own.shape)
        ahead, behind, across = call(pack_kernel, (two, two, one), (core, own, low, high), scalars=True)
        ahead, behind, across, other = lax.optimization_barrier((ahead, behind, across, other))
        across = rotated(across, 2, True)
        return (own, low, high, rotated(ahead, 1), rotated(behind, -1), across), other

    send_a, slope = call(
        functools.partial(first_kernel, nodes, cap),
        (shape((slots, width)), shape((2, slots, units))),
        (ids_a, gate_a, grads_a[0], saved_a[0, 0]),
        flops=2 * slots * tokens * width,
        limit=VMEM_WHOLE,
    )
    rows_a = exchange(send_a, "node")
    send_b = dispatch(ids_b, gate_b, inputs_b[0], False)
    table_a = combine_table(ids_a, gate_a, True)
    table_b = combine_table(ids_b, gate_b, False)
    slopes = lax.all_gather(slope, "local", axis=0, tiled=True).reshape(locals_, 2, slots, units)
    send_b, w_in, table_a, table_b = lax.optimization_barrier((send_b, w_in, table_a, table_b))
    rows_b = exchange(send_b, "node")
    ahead, behind, across, own = partials(grad_hidden_kernel, (slots, units), rows_a, w_out)
    across = rotated(across, -2, True)
    ahead = rotated(ahead, 1)
    behind = rotated(behind, -1)
    half = 2
    part_b = call(
        up_kernel,
        shape((locals_, 2, slots, units)),
        (rows_b, w_in),
        flops=4 * slots * width * units * locals_,
        grid=(locals_ // half,),
        in_specs=[
            pl.BlockSpec((slots, width), lambda i: (0, 0)),
            pl.BlockSpec((2, width, half * units), lambda i: (0, 0, i)),
        ],
        out_specs=pl.BlockSpec((half, 2, slots, units), lambda i: (i, 0, 0, 0)),
    )
    ahead, behind, across, part_b, slopes = lax.optimization_barrier((ahead, behind, across, part_b, slopes))
    plus, minus = relay_sum(own, ahead, behind, across)
    pre_b = lax.psum_scatter(
        part_b.reshape(locals_, 2 * slots, units), "local", scatter_dimension=0, tiled=True
    ).reshape(2, slots, units)
    sums_a = (own, ahead, behind, rotated(plus, 2), rotated(minus, -2))
    grad_hidden = call(grad_sum_kernel, shape((slots, units)), sums_a, flops=10**6)
    grad_hidden, pre_b = gather_local(grad_hidden, pre_b)
    result_a = call(
        input_grad_kernel,
        shape((slots, width)),
        (place, *grad_hidden, slopes, w_in),
        flops=4 * slots * width * units * locals_,
        scalars=True,
    )
    hidden = call(activate_kernel, shape((slots, units)), (pre_b,), flops=10**6, limit=VMEM_WHOLE)
    hidden_all = lax.all_gather(hidden, "local", axis=0, tiled=True).reshape(locals_, slots, units)
    result_b = call(
        down_kernel,
        shape((slots, width)),
        (hidden_all, w_out),
        flops=2 * slots * width * units * locals_,
        limit=VMEM_WHOLE,
    )
    returned_a = exchange(result_a, "node")
    returned_a, result_b = lax.optimization_barrier((returned_a, result_b))
    returned_b = exchange(result_b, "node")
    input_grad = combine(table_a, returned_a)
    grads_prev = shifted(input_grad[None], "section", -1)
    outputs = combine(table_b, returned_b)
    return (outputs[None], grads_prev)


def solution(mesh):
    return jax.shard_map(
        body,
        mesh=mesh,
        in_specs=(
            P("section", "node", "local"),
            P("section", "node", "local"),
            P("section", "node", None),
            P("section", "node", None),
            P("section", "node", None),
            P("section", "node", None),
            P("section", "node", "local", None, None),
            P("section", "node", None, "local"),
            P("section", "node", None, "local", None),
        ),
        out_specs=(P("section", "node", "local"), P("section", "node", "local")),
        check_vma=False,
    )
```
